128 devices in a mesh: dp: 64 (over y_lo, x, z, core), tensor: 2 (over y_hi).
Axes of the slice: x: 4, y: 4 (y_hi: 2, y_lo: 2; y = y_hi * 2 + y_lo), z: 4, core: 2. Of those that a mesh axis runs over, the one named last changes fastest.
Arguments:
- hidden_in: bfloat16 [32768, 1024], P(('dp', 'tensor')), may hold values from -6 to 6
- lengths: int32 [64, 4], P('dp'), may hold values from 1 to 509, as said below
- cotangent: bfloat16 [32768, 1024], P(('dp', 'tensor')), may hold values from -6 to 6
- norm_in: float32 [2, 1024], replicated, may hold values from 0.5 to 1.5
- norm_mid: float32 [2, 1024], replicated, may hold values from 0.5 to 1.5
- query_w: bfloat16 [2, 1024, 512], P(None, 'dp', 'tensor'), may hold values from -0.1875 to 0.1875
- key_w: bfloat16 [2, 1024, 512], P(None, 'dp', 'tensor'), may hold values from -0.1875 to 0.1875
- value_w: bfloat16 [2, 1024, 1024], P(None, 'dp', 'tensor'), may hold values from -0.1875 to 0.1875
- gate_w: bfloat16 [2, 1024, 1024], P(None, 'dp', 'tensor'), may hold values from -0.1875 to 0.1875
- out_w: bfloat16 [2, 1024, 1024], P(None, 'dp', 'tensor'), may hold values from -0.1875 to 0.1875
- low_down: bfloat16 [2, 1024, 16], replicated, may hold values from -0.1875 to 0.1875
- low_up: float32 [2, 16, 512], replicated, may hold values from -1.5 to 1.5
- decay_bias: float32 [2, 512], replicated, may hold values from 0 to 4
- group_gain: float32 [2, 256], replicated, may hold values from 0.1 to 1.9
- ffn_gate: bfloat16 [2, 1024, 2816], P(None, 'dp', 'tensor'), may hold values from -0.1875 to 0.1875
- ffn_up: bfloat16 [2, 1024, 2816], P(None, 'dp', 'tensor'), may hold values from -0.1875 to 0.1875
- ffn_down: bfloat16 [2, 1024, 2816], P(None, 'dp', 'tensor'), may hold values from -0.109375 to 0.109375
Outputs:
- output: float32 [32768, 1024], P(('dp', 'tensor'))
- input_grad: float32 [32768, 1024], P(('dp', 'tensor'))
- grad_norm_in: float32 [2, 1024], replicated
- grad_norm_mid: float32 [2, 1024], replicated
- grad_query_w: float32 [2, 1024, 512], P(None, 'dp', 'tensor')
- grad_key_w: float32 [2, 1024, 512], P(None, 'dp', 'tensor')
- grad_value_w: float32 [2, 1024, 1024], P(None, 'dp', 'tensor')
- grad_gate_w: float32 [2, 1024, 1024], P(None, 'dp', 'tensor')
- grad_out_w: float32 [2, 1024, 1024], P(None, 'dp', 'tensor')
- grad_low_down: float32 [2, 1024, 16], replicated
- grad_low_up: float32 [2, 16, 512], replicated
- grad_decay_bias: float32 [2, 512], replicated
- grad_group_gain: float32 [2, 256], replicated
- grad_ffn_gate: float32 [2, 1024, 2816], P(None, 'dp', 'tensor')
- grad_ffn_up: float32 [2, 1024, 2816], P(None, 'dp', 'tensor')
- grad_ffn_down: float32 [2, 1024, 2816], P(None, 'dp', 'tensor')
The draws below stay inside these ranges and needn't reach their ends.
Inputs may be any that keep to these rules, and one draw needn't show every extreme that they name: Each slot's lengths are at least 1 and sum to between 257 and 512; some slot sums to exactly 512, and in it the last document has 509 positions; no document of a slot ends exactly at position 256, so one document covers positions 255 and 256.
All inputs are finite; a program needn't handle non-finite values.
Results may differ from the reference program's by a relative error of at most 0.035.
Values may be sent and summed in bfloat16 or wider, within the bound.
No kernel may reach another device: no remote copies, remote signals or barrier semaphores. Data moves between devices by JAX's collectives and lax.ppermute only.
A program may use at most 320 MiB of HBM per device.

```python
import jax
import jax.numpy as jnp
from jax import lax

D = 1024
HEADS = 4
HEAD_V = 256
FF = 2816
RANK = 16
SPAN = 64
LAYERS = 2
DOCS = 4
SLOT = 512
KEY = 512
VAL = 1024
SLOTS = 64
TOKENS = 32768


def draw_lengths(key, part):
    key = jax.random.fold_in(key, 11)
    key_used, key_full, key_cut = jax.random.split(key, 3)
    half_slot = SLOT // 2
    used = jax.random.randint(key_used, (SLOTS,), half_slot + 1, SLOT + 1)
    full_slot = jax.random.randint(key_full, (), 0, SLOTS)
    is_full = jnp.arange(SLOTS) == full_slot
    used = jnp.where(is_full, SLOT, used).astype(jnp.int32)
    spots = jnp.arange(1, SLOT, dtype=jnp.int32)
    noise = jax.random.randint(key_cut, (SLOTS, SLOT - 1), 0, 1 << 16)
    score = noise * SLOT + spots[None, :]
    barred = (spots[None, :] >= used[:, None]) | (spots[None, :] == half_slot)
    score = jnp.where(barred, (1 << 30) + spots[None, :], score)
    order = jnp.argsort(score, axis=1, stable=True)[:, :DOCS - 1]
    cuts = jnp.sort(spots[order], axis=1)
    first_cuts = jnp.arange(1, DOCS, dtype=jnp.int32)
    cuts = jnp.where(is_full[:, None], first_cuts[None, :], cuts).astype(jnp.int32)
    bounds = jnp.concatenate([jnp.zeros((SLOTS, 1), jnp.int32), cuts, used[:, None]], axis=1)
    return (bounds[:, 1:] - bounds[:, :-1]).astype(jnp.int32)


def levels(stream_key, extent, cuts, low, high):
    level = 1.0
    for position, blocks in cuts:
        heights = jax.random.uniform(jax.random.fold_in(jax.random.fold_in(stream_key, 6), position), (blocks,), jnp.float32, low / len(cuts), high / len(cuts))
        level = level * jnp.repeat(jnp.exp(heights), extent[position] // blocks).reshape((-1,) + (1,) * (len(extent) - 1 - position))
    return level


def bell_draw(key, dims, deviation, most, cuts=(), kind=jnp.bfloat16):
    entries = deviation * jax.random.normal(key, dims, jnp.float32)
    if cuts:
        entries = entries * levels(key, dims, cuts, -0.22, 0.18)
    return jnp.clip(entries, -most, most).astype(kind)


def setup_inputs(seed: int = 0) -> dict:
    seeds = jax.random.split(jax.random.key(seed), 18)
    hidden_in = bell_draw(seeds[0], (TOKENS, D), 1.0, 6.0, ((0, 128),))
    lengths = draw_lengths(jax.random.fold_in(seeds[17], 71), 0)
    cotangent = bell_draw(seeds[2], (TOKENS, D), 1.0, 6.0, ((0, 128),))
    norm_in = jnp.clip(1.0 + 0.1 * jax.random.normal(seeds[3], (LAYERS, D), jnp.float32), 0.5, 1.5)
    norm_mid = jnp.clip(1.0 + 0.1 * jax.random.normal(seeds[4], (LAYERS, D), jnp.float32), 0.5, 1.5)
    query_w = bell_draw(seeds[5], (LAYERS, D, KEY), D ** -0.5, 0.1875, ((1, 64), (2, 2)))
    key_w = bell_draw(seeds[6], (LAYERS, D, KEY), D ** -0.5, 0.1875, ((1, 64), (2, 2)))
    value_w = bell_draw(seeds[7], (LAYERS, D, VAL), D ** -0.5, 0.1875, ((1, 64), (2, 2)))
    gate_w = bell_draw(seeds[8], (LAYERS, D, VAL), D ** -0.5, 0.1875, ((1, 64), (2, 2)))
    out_w = bell_draw(seeds[9], (LAYERS, D, VAL), VAL ** -0.5, 0.1875, ((1, 64), (2, 2)))
    low_down = bell_draw(seeds[10], (LAYERS, D, RANK), D ** -0.5, 0.1875)
    low_up = bell_draw(seeds[11], (LAYERS, RANK, KEY), RANK ** -0.5, 1.5, (), jnp.float32)
    decay_bias = jnp.clip(jax.random.uniform(seeds[12], (LAYERS, KEY), jnp.float32, 0.0, 4.0), 0.0, 4.0)
    group_gain = jnp.clip(1.0 + 0.18 * jax.random.normal(seeds[13], (LAYERS, HEAD_V), jnp.float32), 0.1, 1.9)
    ffn_gate = bell_draw(seeds[14], (LAYERS, D, FF), D ** -0.5, 0.1875, ((1, 64), (2, 2)))
    ffn_up = bell_draw(seeds[15], (LAYERS, D, FF), D ** -0.5, 0.1875, ((1, 64), (2, 2)))
    ffn_down = bell_draw(seeds[16], (LAYERS, D, FF), FF ** -0.5, 0.109375, ((1, 64), (2, 2)))
    return dict(hidden_in=hidden_in, lengths=lengths, cotangent=cotangent, norm_in=norm_in, norm_mid=norm_mid, query_w=query_w, key_w=key_w, value_w=value_w, gate_w=gate_w, out_w=out_w, low_down=low_down, low_up=low_up, decay_bias=decay_bias, group_gain=group_gain, ffn_gate=ffn_gate, ffn_up=ffn_up, ffn_down=ffn_down)


@jax.custom_vjp
def low(v):
    return lax.optimization_barrier(v.astype(jnp.bfloat16)).astype(jnp.float32)

@jax.custom_vjp
def low_back(v):
    return v

def low_keep(v):
    return (low(v), None)

def low_pass(kept, grad):
    return (grad,)

def back_keep(v):
    return (v, None)

def back_low(kept, grad):
    return (low(grad),)
low.defvjp(low_keep, low_pass)
low_back.defvjp(back_keep, back_low)
highest = lax.Precision.HIGHEST
norm_eps = 1e-06
group_eps = 1.0
decay_norm = 16.0

def matmul(left, right):
    return jnp.dot(left, right, precision=highest, preferred_element_type=jnp.float32)

def rms_scale(rows_in, gain):
    return rows_in * lax.rsqrt(lax.optimization_barrier(jnp.mean(rows_in * rows_in, axis=-1, keepdims=True)) + norm_eps) * gain

def segment_ids(lengths_row, count):
    bounds = jnp.cumsum(lengths_row).astype(jnp.int32)
    places = jnp.arange(count, dtype=jnp.int32)
    return lax.optimization_barrier(jnp.sum((places[:, None] >= bounds[None, :]).astype(jnp.int32), axis=1))

def linear_mix(queries, key_rows, value_rows, log_decay, seg_ids, span_len):
    row_count, head_count, key_width = queries.shape
    value_width = value_rows.shape[2]
    blocks = row_count // span_len
    shape_keys = (blocks, span_len, head_count, key_width)
    query_b = queries.reshape(shape_keys) * key_width ** (-0.5)
    key_b = key_rows.reshape(shape_keys)
    value_b = value_rows.reshape(blocks, span_len, head_count, value_width)
    places = jnp.arange(span_len)
    lower_mask = (places[:, None] >= places[None, :]).astype(jnp.float32)
    cum_decay = jnp.einsum('ts,cshd->cthd', lower_mask, log_decay.reshape(shape_keys), precision=highest)
    query_e = query_b * jnp.exp(cum_decay)
    key_e = key_b * jnp.exp(-cum_decay)
    seg_b = seg_ids.reshape(blocks, span_len)
    same_doc = (seg_b[:, :, None] == seg_b[:, None, :]).astype(jnp.float32) * lower_mask
    scores = jnp.einsum('cthd,cshd->chts', query_e, key_e, precision=highest) * same_doc[:, None]
    inside_part = jnp.einsum('chts,cshe->cthe', scores, value_b, precision=highest)
    last_decay = cum_decay[:, -1]
    last_seg = seg_b[:, -1]
    tail_mask = (seg_b == last_seg[:, None]).astype(jnp.float32)
    key_tail = key_b * jnp.exp(last_decay[:, None] - cum_decay) * tail_mask[:, :, None, None]
    added_state = jnp.einsum('cshd,cshe->chde', key_tail, value_b, precision=highest)
    prev_seg = jnp.concatenate([jnp.full((1,), -1, seg_b.dtype), last_seg[:-1]])
    keep_state = (prev_seg == last_seg).astype(jnp.float32)
    start_mask = (seg_b == prev_seg[:, None]).astype(jnp.float32)

    def advance(carry_state, pieces):
        query_c, added_c, decay_c, keep_c, mask_c = pieces
        from_state = jnp.einsum('thd,hde->the', query_c, carry_state, precision=highest) * mask_c[:, None, None]
        carry_state = carry_state * (keep_c * jnp.exp(decay_c))[:, :, None] + added_c
        return (carry_state, from_state)
    start_state = jnp.zeros((head_count, key_width, value_width), jnp.float32)
    _, carried = lax.scan(advance, start_state, (query_e, added_state, last_decay, keep_state, start_mask))
    return (inside_part + carried).reshape(row_count, head_count, value_width)

def mixer_core(queries, key_rows, value_rows, gates, logits, group_gain, seg_ids, head_count, span_len):
    row_count = queries.shape[0]
    key_width = queries.shape[1] // head_count
    value_width = value_rows.shape[1] // head_count
    log_decay = jax.nn.log_sigmoid(logits) / decay_norm
    mixed = linear_mix(queries.reshape(row_count, head_count, key_width), key_rows.reshape(row_count, head_count, key_width), value_rows.reshape(row_count, head_count, value_width), log_decay.reshape(row_count, head_count, key_width), seg_ids, span_len)
    normed = mixed * lax.rsqrt(lax.optimization_barrier(jnp.mean(mixed * mixed, axis=-1, keepdims=True)) + group_eps) * group_gain
    gated = normed * jax.nn.silu(gates.reshape(row_count, head_count, value_width))
    return gated.reshape(row_count, head_count * value_width)

def reference(hidden_in, lengths, cotangent, norm_in, norm_mid, query_w, key_w, value_w, gate_w, out_w, low_down, low_up, decay_bias, group_gain, ffn_gate, ffn_up, ffn_down):
    seg_all = jax.vmap(lambda row: segment_ids(row, SLOT))(lengths)
    valid = (seg_all < DOCS).astype(jnp.float32).reshape(TOKENS, 1)
    params = tuple((array.astype(jnp.float32) for array in (norm_in, norm_mid, query_w, key_w, value_w, gate_w, out_w, low_down, low_up, decay_bias, group_gain, ffn_gate, ffn_up, ffn_down)))

    def forward(hidden, weights):
        gain_in, gain_mid, w_query, w_key, w_value, w_gate, w_out, w_down, w_up, bias_all, gain_group, w_fgate, w_fup, w_fdown = weights
        for layer_index in range(LAYERS):
            normed = low(rms_scale(hidden, gain_in[layer_index]))
            queries = low(low_back(matmul(normed, w_query[layer_index])))
            key_rows = low(low_back(matmul(normed, w_key[layer_index])))
            value_rows = low(low_back(matmul(normed, w_value[layer_index])))
            gates = low_back(matmul(normed, w_gate[layer_index]))
            latent = matmul(normed, w_down[layer_index])
            logits = matmul(latent, w_up[layer_index]) + bias_all[layer_index]
            layer_gain = gain_group[layer_index]

            def one_slot(pieces):
                return mixer_core(pieces[0], pieces[1], pieces[2], pieces[3], pieces[4], layer_gain, pieces[5], HEADS, SPAN)
            mixed_rows = lax.map(jax.checkpoint(one_slot), (queries.reshape(SLOTS, SLOT, KEY), key_rows.reshape(SLOTS, SLOT, KEY), value_rows.reshape(SLOTS, SLOT, VAL), gates.reshape(SLOTS, SLOT, VAL), logits.reshape(SLOTS, SLOT, KEY), seg_all))
            out_rows = low(mixed_rows.reshape(TOKENS, VAL))
            hidden = hidden + low_back(matmul(out_rows, w_out[layer_index].T))
            normed_mid = low(rms_scale(hidden, gain_mid[layer_index]))
            gate_pre = low_back(matmul(normed_mid, w_fgate[layer_index]))
            up_pre = low_back(matmul(normed_mid, w_fup[layer_index]))
            acted = low(jax.nn.silu(gate_pre) * up_pre)
            hidden = hidden + low_back(matmul(acted, w_fdown[layer_index].T))
        return hidden
    output, pull_back = jax.vjp(forward, hidden_in.astype(jnp.float32), params)
    input_grad, grads = pull_back(cotangent.astype(jnp.float32) * valid)
    return (output, input_grad, grads[0], grads[1], grads[2], grads[3], grads[4], grads[5], grads[6], grads[7], grads[8], grads[9], grads[10], grads[11], grads[12], grads[13])
```

```python
from functools import partial

import jax
import jax.numpy as jnp
from jax import lax
from jax.experimental import pallas as pl
from jax.experimental.pallas import tpu as pltpu
from jax.sharding import Mesh, PartitionSpec as P

LAYERS = 2
HEADS = 4
SPAN = 64
ROWS = 256
D = 1024
KD = 128
VD = 256
FINE = ("yl", "x", "z", "c", "yh")
PLANE = {"x": ("yh", "yl", "z"), "y": ("x", "z"), "z": ("yh", "yl", "x")}
GROUPS = ("x", "z", "y")
bf = jnp.bfloat16
f32 = jnp.float32
highest = lax.Precision.HIGHEST
norm_eps = 1e-06
group_eps = 1.0
decay_norm = 16.0
scale = KD**-0.5
NN = (((1,), (0,)), ((), ()))
NT = (((1,), (1,)), ((), ()))
TN = (((0,), (0,)), ((), ()))


def dot(a, b, dims=NN, precision=None):
    return lax.dot_general(a, b, dims, precision=precision, preferred_element_type=f32)


def call(kernel, out_shape, *, flops=0, moved=0, vmem=48, **kw):
    return pl.pallas_call(
        kernel,
        out_shape=out_shape,
        compiler_params=pltpu.CompilerParams(vmem_limit_bytes=vmem << 20),
        cost_estimate=pl.CostEstimate(flops=flops, bytes_accessed=moved, transcendentals=0),
        **kw,
    )


def shape(*dims, dtype=f32):
    return jax.ShapeDtypeStruct(dims, dtype)


def swap(a):
    return lax.ppermute(a, "c", [(0, 1), (1, 0)])


def ring(a, axis):
    if axis == "y":
        names = ("yl", "c", "yh")
        place = lambda i, c: ((i % 2) * 2 + c) * 2 + i // 2
    else:
        names = (axis, "c")
        place = lambda i, c: i * 2 + c
    pairs = [
        (place(i, c), place((i + 1 - 2 * c) % 4, c)) for i in range(4) for c in range(2)
    ]
    return lax.ppermute(a, names, pairs)


def plane_gather(s, axis):
    b = jnp.broadcast_to(s[None], (16, *s.shape))
    return lax.all_to_all(b, PLANE[axis], 0, 0, tiled=True)


def plane_sum(t, axis):
    r = lax.all_to_all(t, PLANE[axis], 0, 0, tiled=True)
    return jnp.sum(r.astype(f32), axis=0)


def axis_gather(p, axis):
    b0 = jnp.stack([p, swap(p)])
    t1 = ring(b0, axis)
    t2 = ring(t1[0], axis)
    lead = (256,) if axis == "y" else (2, 128)
    pieces = (b0, t1, swap(t1), t2, swap(t2))
    return tuple(a.reshape(*((2,) if a.ndim == 4 else ()), *lead, a.shape[-1]) for a in pieces)


def axis_sum(parts, axis):
    u1, u2, u0 = (a.reshape(*a.shape[: a.ndim - (2 if axis == "y" else 3)], 16, 16, a.shape[-1]) for a in parts)
    r2 = ring(u2, axis)
    u1 = jnp.stack([(u1[0].astype(f32) + r2.astype(f32)).astype(bf), u1[1]])
    r1 = ring(u1, axis)
    far = swap(r1[1])
    return (u0.astype(f32) + r1[0].astype(f32) + far.astype(f32)).astype(bf)


def rows_of(refs, pick):
    b0, t1, t1p, t2, t2p = refs
    return jnp.concatenate(
        [pick(b0, 0), pick(b0, 1), pick(t1, 0), pick(t1, 1), pick(t1p, 0), pick(t1p, 1), pick(t2, None), pick(t2p, None)],
        axis=0,
    )


def half_of(ref, part):
    return ref[0] if part is None else ref[part, 0]


def half_specs(width):
    two = pl.BlockSpec((2, 1, 128, width), lambda h: (0, h, 0, 0))
    one = pl.BlockSpec((1, 128, width), lambda h: (h, 0, 0))
    return [two, two, two, one, one]


def whole(*dims):
    return pl.BlockSpec(dims, lambda h: (0,) * len(dims))


def per_half(*dims):
    return pl.BlockSpec((1, *dims), lambda h: (h,) + (0,) * len(dims))


def proj_kernel(x, *refs):
    out = refs[5]
    out[0] = dot(x[...], rows_of(refs[:5], half_of)).astype(out.dtype)


def proj(x, pieces):
    n = pieces[0].shape[-1]
    return call(
        proj_kernel,
        shape(2, ROWS, n, dtype=bf),
        grid=(2,),
        in_specs=[whole(ROWS, D)] + half_specs(n),
        out_specs=per_half(ROWS, n),
        flops=4 * ROWS * D * n,
        moved=4 * D * n,
    )(x, *pieces)


def ffn_kernel(hx, hz, *refs):
    gate = dot(hx[...], rows_of(refs[:5], half_of))
    up = dot(hz[...], rows_of(refs[5:10], half_of))
    gate_out, up_out, acted = refs[10:]
    gate_out[0] = gate.astype(bf)
    up_out[0] = up.astype(bf)
    acted[0] = (gate * jax.nn.sigmoid(gate) * up).astype(bf)


def ffn(hx, hz, px, pz):
    n = px[0].shape[-1]
    return call(
        ffn_kernel,
        (shape(2, ROWS, n, dtype=bf),) * 3,
        grid=(2,),
        in_specs=[whole(ROWS, D)] * 2 + half_specs(n) * 2,
        out_specs=[per_half(ROWS, n)] * 3,
        flops=8 * ROWS * D * n,
        moved=8 * D * n,
    )(hx, hz, *px, *pz)


def spread(value, perm):
    high = value.astype(bf)
    low = (value - high.astype(f32)).astype(bf)
    return dot(high, perm) + dot(low, perm)


def rms(v, gain):
    return v * lax.rsqrt(jnp.mean(v * v, axis=-1, keepdims=True) + norm_eps) * gain


def y_out_kernel(normed, where_, src, x, gain, py, px, pz, *refs):
    b0, t1, t1p, t2, t2p = refs[:5]
    outs = refs[5:]
    h, h1 = where_[0], where_[1]
    own, far = src[h], src[1 - h]
    one, two = src[h1], src[1 - h1]
    d0 = dot(own, b0[0], NT) + dot(far, t2[...], NT)
    d1 = dot(own, b0[1], NT) + dot(far, t2p[...], NT)
    d2 = dot(one, t1[0], NT) + dot(two, t1p[1], NT)
    d3 = dot(one, t1[1], NT) + dot(two, t1p[0], NT)
    total = x[...] + spread(jnp.concatenate([d0, d1, d2, d3], axis=1), py[...])
    outs[0][...] = total
    if normed:
        hn = rms(total, gain[...]).astype(bf)
        outs[1][...] = hn
        outs[2][...] = dot(hn, px[...], NT).astype(bf)
        outs[3][...] = dot(hn, pz[...], NT).astype(bf)


def y_out(where_, src, x, gain, perms, pieces, normed=True):
    n = pieces[0].shape[-1]
    vm = pl.BlockSpec(memory_space=pltpu.VMEM)
    outs = (shape(ROWS, D),) + ((shape(ROWS, D, dtype=bf),) * 3 if normed else ())
    return call(
        partial(y_out_kernel, normed),
        outs,
        in_specs=[pl.BlockSpec(memory_space=pltpu.SMEM)] + [vm] * (len(pieces) + 6),
        out_specs=tuple([vm] * len(outs)),
        flops=4 * ROWS * D * n + 8 * ROWS * D * D,
        moved=4 * D * n + 8 * D * D,
    )(where_, src, x, gain, perms["y"], perms["x"], perms["z"], *pieces)


def norm_kernel(x, gain, px, pz, hn_out, hx, hz):
    hn = rms(x[...], gain[...]).astype(bf)
    hn_out[...] = hn
    hx[...] = dot(hn, px[...], NT).astype(bf)
    hz[...] = dot(hn, pz[...], NT).astype(bf)


def norm_rows(x, gain, perms):
    return call(
        norm_kernel,
        (shape(ROWS, D, dtype=bf),) * 3,
        flops=4 * ROWS * D * D,
        moved=6 * D * D,
    )(x, gain, perms["x"], perms["z"])


def y_back_kernel(acting, where_, g, py, *refs):
    b0, t1, t1p, t2, t2p = refs[:5]
    h, h1 = where_[0], where_[1]
    same = h == h1
    gy = dot(g[...].astype(bf), py[...], NT).astype(bf)
    near, far = gy[:, :512], gy[:, 512:]
    joined = lambda a, b: jnp.concatenate([a, b], axis=0)
    part_a = dot(near, joined(b0[0], b0[1]))
    part_b = dot(near, joined(t2[...], t2p[...]))
    part_c = dot(far, joined(t1[0], t1[1]))
    part_d = dot(far, joined(t1p[1], t1p[0]))
    pick_c = jnp.where(same, 1.0, 0.0)
    pick_d = 1.0 - pick_c
    halves = (
        (h, part_a + pick_c * part_c + pick_d * part_d),
        (1 - h, part_b + pick_d * part_c + pick_c * part_d),
    )
    if acting:
        gate_in, up_in, gy_out, dgate, dup = refs[5:]
        gy_out[...] = gy
        for place, da in halves:
            gate = gate_in[place].astype(f32)
            up = up_in[place].astype(f32)
            sg = jax.nn.sigmoid(gate)
            dgate[place] = (da * up * sg * (1.0 + gate * (1.0 - sg))).astype(bf)
            dup[place] = (da * gate * sg).astype(bf)
    else:
        gy_out, out = refs[5:]
        gy_out[...] = gy
        for place, da in halves:
            out[place] = da


def y_back(where_, g, perms, pieces, saved=None):
    n = pieces[0].shape[-1]
    vm = pl.BlockSpec(memory_space=pltpu.VMEM)
    extra = () if saved is None else tuple(saved)
    outs = (shape(ROWS, D, dtype=bf),)
    outs += (shape(2, ROWS, n),) if saved is None else (shape(2, ROWS, n, dtype=bf),) * 2
    return call(
        partial(y_back_kernel, saved is not None),
        outs,
        in_specs=[pl.BlockSpec(memory_space=pltpu.SMEM)] + [vm] * (7 + len(extra)),
        out_specs=tuple([vm] * len(outs)),
        flops=4 * ROWS * D * n + 2 * ROWS * D * D,
        moved=4 * D * n + 2 * D * D,
    )(where_, g, perms["y"], *pieces, *extra)


def norm_back(v, gain, d_out):
    r = lax.rsqrt(jnp.mean(v * v, axis=-1, keepdims=True) + norm_eps)
    u = d_out * gain
    d_v = r * u - v * (r * r * r) * jnp.mean(u * v, axis=-1, keepdims=True)
    return d_v, jnp.sum(d_out * v * r, axis=0, keepdims=True)


def x_back_kernel(low, dx, dz, x, gain, g, px, pz, *refs):
    h = pl.program_id(0)
    rest = refs[10:]
    if low:
        d_logits, low_up, low_down = rest[:3]
        rest = rest[3:]
    g_out, gain_out = rest[:2]
    acc_x, acc_z = rest[-2:]
    part_x = dot(dx[0], rows_of(refs[:5], half_of), NT)
    part_z = dot(dz[0], rows_of(refs[5:10], half_of), NT)

    @pl.when(h == 0)
    def _():
        acc_x[...] = part_x
        acc_z[...] = part_z

    @pl.when(h == 1)
    def _():
        d_hn = spread(acc_x[...] + part_x, px[...]) + spread(acc_z[...] + part_z, pz[...])
        if low:
            d_latent = dot(d_logits[...], low_up[...], NT, highest)
            rest[2][...] = d_latent
            d_hn = d_hn + dot(d_latent, low_down[...], NT, highest)
        d_v, d_gain = norm_back(x[...], gain[...], d_hn)
        g_out[...] = g[...] + d_v
        gain_out[...] = d_gain


def x_back(dx, dz, x, gain, g, perms, px, pz, low=None):
    n = px[0].shape[-1]
    outs = (shape(ROWS, D), shape(1, D))
    out_specs = [whole(ROWS, D), whole(1, D)]
    extra, extra_specs = (), []
    if low is not None:
        extra = tuple(low)
        extra_specs = [whole(*a.shape) for a in low]
        outs += (shape(ROWS, 16),)
        out_specs.append(whole(ROWS, 16))
    return call(
        partial(x_back_kernel, low is not None),
        outs,
        grid=(2,),
        in_specs=[per_half(ROWS, n)] * 2
        + [whole(ROWS, D), whole(1, D), whole(ROWS, D), whole(D, D), whole(D, D)]
        + half_specs(n) * 2
        + extra_specs,
        out_specs=out_specs,
        scratch_shapes=[pltpu.VMEM((ROWS, D), f32)] * 2,
        flops=8 * ROWS * D * n + 8 * ROWS * D * D,
        moved=8 * D * n + 4 * D * D,
    )(dx, dz, x, gain, g, perms["x"], perms["z"], *px, *pz, *extra)


def x_weight_kernel(a, ar, d, dr, u1, u2, u0):
    r = (dot(a[...], d[0], TN) + dot(ar[...], dr[0], TN)).astype(bf)
    u1[0, 0] = r[:128]
    u1[1, 0] = r[128:256]
    u2[0] = r[256:384]
    u0[0] = r[384:]


def cols(a, *blocks, width=128):
    return jnp.concatenate([a[:, b * width : (b + 1) * width] for b in blocks], axis=1)


def x_weight(hx, hx_far, d, d_far):
    n = d.shape[-1]
    one = per_half(128, n)
    return call(
        x_weight_kernel,
        (shape(2, 2, 128, n, dtype=bf), shape(2, 128, n, dtype=bf), shape(2, 128, n, dtype=bf)),
        grid=(2,),
        in_specs=[whole(ROWS, 512)] * 2 + [per_half(ROWS, n)] * 2,
        out_specs=[pl.BlockSpec((2, 1, 128, n), lambda h: (0, h, 0, 0)), one, one],
        flops=4 * ROWS * D * n,
        moved=2 * D * n,
    )(hx, hx_far, d, d_far)


def y_weight_kernel(where_, a, ar, d, dr, u1, u2, u0):
    h, h2 = where_[0], 1 - where_[1]
    first = lambda place: dot(a[:, :256], d[place], TN) + dot(ar[:, :256], dr[place], TN)
    u0[...] = first(h).astype(bf)
    u2[...] = first(1 - h).astype(bf)
    r = dot(a[:, 256:], d[h2], TN) + dot(ar[:, 256:], dr[h2], TN)
    u1[0] = r[:256].astype(bf)
    u1[1] = r[256:].astype(bf)


def y_weight(where_, gy, gy_far, d, d_far):
    n = d.shape[-1]
    vm = pl.BlockSpec(memory_space=pltpu.VMEM)
    return call(
        y_weight_kernel,
        (shape(2, 256, n, dtype=bf), shape(256, n, dtype=bf), shape(256, n, dtype=bf)),
        in_specs=[pl.BlockSpec(memory_space=pltpu.SMEM)] + [vm] * 4,
        out_specs=(vm, vm, vm),
        flops=4 * ROWS * D * n,
        moved=2 * D * n,
    )(where_, gy, gy_far, d, d_far)


def log_sigmoid(v):
    return jnp.minimum(v, 0.0) - jnp.log1p(jnp.exp(-jnp.abs(v)))


def decays(logits):
    ld = log_sigmoid(logits) / decay_norm
    r = lax.broadcasted_iota(jnp.int32, (ROWS, ROWS), 0)
    c = lax.broadcasted_iota(jnp.int32, (ROWS, ROWS), 1)
    lower = ((r >= c) & (r // SPAN == c // SPAN)).astype(f32)
    cum = dot(lower, ld, NN, highest)
    blocks = [cum[i * SPAN : (i + 1) * SPAN] for i in range(4)]
    ends = [b[SPAN - 1 :] for b in blocks]
    return blocks, ends


def run_sum(ends, start, stop):
    total = jnp.zeros_like(ends[0])
    for i in range(start, stop):
        total = total + ends[i]
    return total


def key_factors(blocks, ends, i):
    parts = [jnp.exp((ends[j] - blocks[j]) + run_sum(ends, j + 1, i)) for j in range(i)]
    parts.append(jnp.exp(-blocks[i]))
    return jnp.concatenate(parts, axis=0)


def allowed(segr, segc, i):
    rows_i = segr[i * SPAN : (i + 1) * SPAN]
    count = (i + 1) * SPAN
    r = lax.broadcasted_iota(jnp.int32, (SPAN, count), 0) + i * SPAN
    c = lax.broadcasted_iota(jnp.int32, (SPAN, count), 1)
    return (r >= c) & (rows_i == segc[:, :count])


def start_factors(blocks, ends):
    return jnp.concatenate([jnp.exp(blocks[i] + run_sum(ends, 0, i)) for i in range(4)], axis=0)


def tail_factors(blocks, ends):
    return jnp.concatenate([jnp.exp((ends[i] - blocks[i]) + run_sum(ends, i + 1, 4)) for i in range(4)], axis=0)


def mix_kernel(q, k, v, logits, segr, segc, out, state, state_q):
    blocks, ends = decays(logits[...])
    kf = k[0].astype(f32)
    qf = q[0].astype(f32) * scale
    segr, segc = segr[...], segc[...]
    tail = tail_factors(blocks, ends)
    tail_k = jnp.where(segr == segr[ROWS - 1 :], kf * tail, 0.0).astype(bf)
    state[0] = dot(tail_k, v[0], TN).astype(bf)
    state_q[0] = jnp.where(segr == segr[:1], qf * start_factors(blocks, ends), 0.0).astype(bf)
    for i in range(4):
        count = (i + 1) * SPAN
        qe = (qf[i * SPAN : count] * jnp.exp(blocks[i])).astype(bf)
        ke = (kf[:count] * key_factors(blocks, ends, i)).astype(bf)
        p = jnp.where(allowed(segr, segc, i), dot(qe, ke, NT), 0.0).astype(bf)
        out[0, i * SPAN : count] = dot(p, v[0, :count])


def head_cols(width, first=0):
    return pl.BlockSpec((1, ROWS, width), lambda t: (t // 2, 0, first + t % 2))


def by_head(*dims):
    return pl.BlockSpec((1, *dims), lambda t: (t,) + (0,) * len(dims))


def mix(qv, kg, logits, segr, segc):
    return call(
        mix_kernel,
        (
            shape(2, ROWS, 2 * VD),
            shape(HEADS, KD, VD, dtype=bf),
            shape(HEADS, ROWS, KD, dtype=bf),
        ),
        grid=(HEADS,),
        in_specs=[
            head_cols(KD),
            head_cols(KD),
            head_cols(VD, 1),
            pl.BlockSpec((ROWS, KD), lambda t: (0, t)),
            whole(ROWS, 1),
            whole(1, ROWS),
        ],
        out_specs=[head_cols(VD), by_head(KD, VD), by_head(ROWS, KD)],
        flops=HEADS * 120_000_000,
        moved=4_000_000,
    )(qv, kg, qv, logits, segr, segc)


def gate_kernel(local, state_q, state, g, gain, mixed_out, rows):
    mixed = local[0] + dot(state_q[0], state[0])
    mixed_out[0] = mixed
    gate = g[0].astype(f32)
    on = mixed * lax.rsqrt(jnp.mean(mixed * mixed, axis=-1, keepdims=True) + group_eps) * gain[...]
    rows[0] = (on * gate * jax.nn.sigmoid(gate)).astype(bf)


def gate_rows(local, state_q, state, kg, gain):
    return call(
        gate_kernel,
        (shape(2, ROWS, 2 * VD), shape(2, ROWS, 2 * VD, dtype=bf)),
        grid=(HEADS,),
        in_specs=[head_cols(VD), by_head(ROWS, KD), by_head(KD, VD), head_cols(VD, 1), whole(1, VD)],
        out_specs=[head_cols(VD), head_cols(VD)],
        flops=HEADS * 20_000_000,
        moved=3_000_000,
    )(local, state_q, state, kg, gain)


def mix_back_kernel(
    d_rows, mixed_in, g, gain_in, q, k, v, logits, segr, segc, state_in, state_q_in,
    dg_out, dgain, d_state, dq_out, dk_out, dv_out, net_out,
):
    mixed = mixed_in[0]
    gate = g[0].astype(f32)
    gain = gain_in[...]
    rho = lax.rsqrt(jnp.mean(mixed * mixed, axis=-1, keepdims=True) + group_eps)
    ng = mixed * rho
    sg = jax.nn.sigmoid(gate)
    dr = d_rows[0]
    d_on = dr * gate * sg
    dg_out[0] = (dr * ng * gain * sg * (1.0 + gate * (1.0 - sg))).astype(bf)
    dgain[0] = jnp.sum(d_on * ng, axis=0, keepdims=True)
    w = d_on * gain
    do = (rho * (w - ng * jnp.mean(w * ng, axis=-1, keepdims=True))).astype(bf)

    blocks, ends = decays(logits[...])
    kf = k[0].astype(f32)
    qf = q[0].astype(f32) * scale
    segr, segc = segr[...], segc[...]
    sq = state_q_in[0]
    d_state[0] = dot(sq, do, TN).astype(bf)
    from_state = dot(do, state_in[0], NT)
    start = jnp.where(segr == segr[:1], start_factors(blocks, ends), 0.0) * scale
    dq_state = from_state * start
    net_state = from_state * sq.astype(f32)
    dk = jnp.zeros((ROWS, KD), f32)
    dv = jnp.zeros((ROWS, VD), f32)
    net_k = jnp.zeros((ROWS, KD), f32)
    nets = []
    grow = lambda a: a if a.shape[0] == ROWS else jnp.concatenate(
        [a, jnp.zeros((ROWS - a.shape[0], a.shape[1]), f32)], axis=0
    )
    for i in range(4):
        count = (i + 1) * SPAN
        here = slice(i * SPAN, count)
        eb = jnp.exp(blocks[i])
        qe = (qf[here] * eb).astype(bf)
        factors = key_factors(blocks, ends, i)
        ke = (kf[:count] * factors).astype(bf)
        keep = allowed(segr, segc, i)
        p = jnp.where(keep, dot(qe, ke, NT), 0.0).astype(bf)
        dp = jnp.where(keep, dot(do[here], v[0, :count], NT), 0.0).astype(bf)
        dv = dv + grow(dot(p, do[here], TN))
        dqe = dot(dp, ke)
        dq_out[0, here] = (dqe * eb * scale + dq_state[here]).astype(bf)
        nets.append(dqe * qe.astype(f32) + net_state[here])
        dke = dot(dp, qe, TN)
        dk = dk + grow(dke * factors)
        net_k = net_k + grow(dke * ke.astype(f32))
    dk_out[0] = dk
    dv_out[0] = dv
    net_out[0] = jnp.concatenate(nets, axis=0) - net_k


def mix_back(d_rows, mixed, qv, kg, gain, logits, segr, segc, state, state_q):
    return call(
        mix_back_kernel,
        (
            shape(2, ROWS, 2 * VD, dtype=bf),
            shape(HEADS, 1, VD),
            shape(HEADS, KD, VD, dtype=bf),
            shape(2, ROWS, 2 * KD, dtype=bf),
            shape(HEADS, ROWS, KD),
            shape(HEADS, ROWS, VD),
            shape(HEADS, ROWS, KD),
        ),
        grid=(HEADS,),
        in_specs=[
            head_cols(VD),
            head_cols(VD),
            head_cols(VD, 1),
            whole(1, VD),
            head_cols(KD),
            head_cols(KD),
            head_cols(VD, 1),
            pl.BlockSpec((ROWS, KD), lambda t: (0, t)),
            whole(ROWS, 1),
            whole(1, ROWS),
            by_head(KD, VD),
            by_head(ROWS, KD),
        ],
        out_specs=[
            head_cols(VD),
            by_head(1, VD),
            by_head(KD, VD),
            head_cols(KD),
            by_head(ROWS, KD),
            by_head(ROWS, VD),
            by_head(ROWS, KD),
        ],
        flops=HEADS * 300_000_000,
        moved=8_000_000,
    )(d_rows, mixed, kg, gain, qv, kg, qv, logits, segr, segc, state, state_q)


def decay_back_kernel(dk_in, dv_in, net, k, v, logits_in, segr, segc, d_state, dk_out, dv_out, d_logits):
    logits = logits_in[...]
    blocks, ends = decays(logits)
    segr, segc = segr[...], segc[...]
    kf = k[0].astype(f32)
    tail = jnp.where(segr == segr[ROWS - 1 :], tail_factors(blocks, ends), 0.0)
    tail_k = (kf * tail).astype(bf)
    ds = d_state[0]
    back = dot(v[0], ds, NT)
    dk_out[0] = (dk_in[0] + back * tail).astype(bf)
    dv_out[0] = (dv_in[0] + dot(tail_k, ds)).astype(bf)
    r = lax.broadcasted_iota(jnp.int32, (ROWS, ROWS), 0)
    c = lax.broadcasted_iota(jnp.int32, (ROWS, ROWS), 1)
    same = segr == segc
    after = jnp.where(same & (c >= r), 1.0, 0.0)
    before = jnp.where(same & (c < r), 1.0, 0.0)
    d_ld = dot(after, net[0], NN, highest) + dot(before, back * tail_k.astype(f32), NN, highest)
    d_logits[...] = d_ld * jax.nn.sigmoid(-logits) / decay_norm


def decay_back(dk, dv, net, qv, kg, logits, segr, segc, d_state):
    return call(
        decay_back_kernel,
        (
            shape(2, ROWS, 2 * KD, dtype=bf),
            shape(2, ROWS, 2 * VD, dtype=bf),
            shape(ROWS, HEADS * KD),
        ),
        grid=(HEADS,),
        in_specs=[
            by_head(ROWS, KD),
            by_head(ROWS, VD),
            by_head(ROWS, KD),
            head_cols(KD),
            head_cols(VD, 1),
            pl.BlockSpec((ROWS, KD), lambda t: (0, t)),
            whole(ROWS, 1),
            whole(1, ROWS),
            by_head(KD, VD),
        ],
        out_specs=[head_cols(KD), head_cols(VD), pl.BlockSpec((ROWS, KD), lambda t: (0, t))],
        flops=HEADS * 100_000_000,
        moved=4_000_000,
    )(dk, dv, net, kg, qv, logits, segr, segc, d_state)


def one_hot(places):
    return (places[:, None] == jnp.arange(D, dtype=jnp.int32)[None, :]).astype(bf)


def permutations():
    yl, x, z, c, yh = (lax.axis_index(a) for a in FINE)
    k = jnp.arange(D, dtype=jnp.int32)
    s = 1 - 2 * c
    step = lambda a: jnp.stack([a, a, a - s, a - s, a + s, a + s, a + 2, a + 2]) % 4
    core = jnp.stack([c, 1 - c, c, 1 - c, 1 - c, c, c, 1 - c])
    pick = lambda table, b: jnp.sum(jnp.where(b[:, None] == jnp.arange(table.shape[0])[None], table[None], 0), axis=1)
    block, r = k // 128, k % 128
    low_y, low_a, rr = r // 64, (r // 16) % 4, r % 16
    index = lambda yl, x, z, c: ((yl * 4 + x) * 4 + z) * 32 + c * 16 + rr
    perms = {
        "x": one_hot(index(low_y, pick(step(x), block), low_a, pick(core, block))),
        "z": one_hot(index(low_y, low_a, pick(step(z), block), pick(core, block))),
    }
    block, r = k // 256, k % 256
    perms["y"] = one_hot(
        index(
            pick(jnp.stack([yl, yl, 1 - yl, 1 - yl]), block),
            r // 64,
            (r // 16) % 4,
            pick(jnp.stack([c, 1 - c, c, 1 - c]), block),
        )
    )
    before = (yh * 2 + yl - s) % 4
    return perms, jnp.stack([yh, before // 2]).astype(jnp.int32)


def local(
    hidden_in, lengths, cotangent, norm_in, norm_mid, query_w, key_w, value_w, gate_w, out_w,
    low_down, low_up, decay_bias, group_gain, ffn_gate, ffn_up, ffn_down,
):
    yh = lax.axis_index("yh")
    perms, where_ = permutations()
    bounds = jnp.cumsum(lengths[0])
    places = jnp.arange(ROWS, dtype=jnp.int32) + yh * ROWS
    seg = jnp.sum((places[:, None] >= bounds[None, :]).astype(jnp.int32), axis=1)
    valid = (seg < lengths.shape[1]).astype(f32)
    segr, segc = seg[:, None], seg[None, :]

    shards = []
    for layer in range(LAYERS):
        shards.append(
            {
                "x": jnp.concatenate([query_w[layer], value_w[layer], ffn_gate[layer]], axis=1),
                "z": jnp.concatenate([key_w[layer], gate_w[layer], ffn_up[layer]], axis=1),
                "y": jnp.concatenate([out_w[layer], ffn_down[layer]], axis=1),
            }
        )
    attn_width = {"x": 768, "z": 768, "y": 512}
    weights = []
    for layer in range(LAYERS):
        planes = {a: plane_gather(shards[layer][a], a) for a in GROUPS}
        attn = {a: axis_gather(planes[a][..., : attn_width[a]], a) for a in GROUPS}
        feed = {a: axis_gather(planes[a][..., attn_width[a] :], a) for a in GROUPS}
        weights.append((attn, feed))

    x = hidden_in.astype(f32)
    hn, hnx, hnz = norm_rows(x, norm_in[:1], perms)
    saved = []
    for layer in range(LAYERS):
        attn, feed = weights[layer]
        qv = proj(hnx, attn["x"])
        kg = proj(hnz, attn["z"])
        latent = dot(hn, low_down[layer])
        logits = dot(latent, low_up[layer], NN, highest) + decay_bias[layer]
        local_mix, state, state_q = mix(qv, kg, logits, segr, segc)
        state = lax.ppermute(state, "yh", [(0, 1)])
        mixed, rows = gate_rows(local_mix, state_q, state, kg, group_gain[layer][None])
        x_mid, hm, hmx, hmz = y_out(where_, rows, x, norm_mid[layer : layer + 1], perms, attn["y"])
        gate_pre, up_pre, acted = ffn(hmx, hmz, feed["x"], feed["z"])
        saved.append((x, hn, hnx, hnz, qv, kg, latent, logits, state, state_q, mixed, rows, x_mid, hmx, hmz, gate_pre, up_pre, acted))
        if layer + 1 < LAYERS:
            x, hn, hnx, hnz = y_out(where_, acted, x_mid, norm_in[layer + 1 : layer + 2], perms, feed["y"])
        else:
            (x,) = y_out(where_, acted, x_mid, norm_in[:1], perms, feed["y"], normed=False)
    output = x

    g = cotangent.astype(f32) * valid[:, None]
    large = [None] * LAYERS
    small = [None] * LAYERS
    for layer in reversed(range(LAYERS)):
        attn, feed = weights[layer]
        x, hn, hnx, hnz, qv, kg, latent, logits, state, state_q, mixed, rows, x_mid, hmx, hmz, gate_pre, up_pre, acted = saved[layer]
        gb, d_gate, d_up = y_back(where_, g, perms, feed["y"], (gate_pre, up_pre))
        g_mid, grad_mid = x_back(d_gate, d_up, x_mid, norm_mid[layer : layer + 1], g, perms, feed["x"], feed["z"])
        mine, theirs = (5, 4, 6, 0), (3, 2, 7, 1)
        y_mine = lambda a: cols(a, 0, 2, 3, width=256)
        y_theirs = lambda a: swap(cols(a, 1, 3, 2, width=256))
        sums = {}
        u = y_weight(where_, y_mine(gb), y_theirs(gb), acted, swap(acted))
        sums["fd"] = axis_sum(u, "y")
        u = x_weight(cols(hmx, *mine), swap(cols(hmx, *theirs)), d_gate, swap(d_gate))
        sums["fg"] = axis_sum(u, "x")
        u = x_weight(cols(hmz, *mine), swap(cols(hmz, *theirs)), d_up, swap(d_up))
        sums["fu"] = axis_sum(u, "z")

        gm, d_rows = y_back(where_, g_mid, perms, attn["y"])
        u = y_weight(where_, y_mine(gm), y_theirs(gm), rows, swap(rows))
        sums["o"] = axis_sum(u, "y")
        d_g, d_gain, d_state, d_q, d_k, d_v, net = mix_back(
            d_rows, mixed, qv, kg, group_gain[layer][None], logits, segr, segc, state, state_q
        )
        d_state = lax.ppermute(d_state, "yh", [(1, 0)])
        d_k, d_v, d_logits = decay_back(d_k, d_v, net, qv, kg, logits, segr, segc, d_state)
        d_qv = jnp.concatenate([d_q, d_v], axis=2)
        d_kg = jnp.concatenate([d_k, d_g], axis=2)
        g, grad_in, d_latent = x_back(
            d_qv, d_kg, x, norm_in[layer : layer + 1], g_mid, perms, attn["x"], attn["z"],
            (d_logits, low_up[layer], low_down[layer].astype(f32)),
        )
        u = x_weight(cols(hnx, *mine), swap(cols(hnx, *theirs)), d_qv, swap(d_qv))
        sums["qv"] = axis_sum(u, "x")
        u = x_weight(cols(hnz, *mine), swap(cols(hnz, *theirs)), d_kg, swap(d_kg))
        sums["kg"] = axis_sum(u, "z")
        large[layer] = {
            "x": (plane_sum(sums["qv"], "x"), plane_sum(sums["fg"], "x")),
            "z": (plane_sum(sums["kg"], "z"), plane_sum(sums["fu"], "z")),
            "y": (plane_sum(sums["o"], "y"), plane_sum(sums["fd"], "y")),
        }
        small[layer] = (
            grad_in[0],
            grad_mid[0],
            dot(hn.astype(f32), d_latent, TN, highest),
            dot(latent, d_logits, TN, highest),
            jnp.sum(d_logits, axis=0),
            jnp.sum(d_gain[:, 0], axis=0),
        )
    input_grad = g

    stacked = [jnp.stack([part[i] for part in small]) for i in range(6)]
    flat = jnp.concatenate([a.reshape(-1) for a in stacked])
    flat = jnp.pad(flat, (0, 128 * 512 - flat.shape[0])).reshape(128, 4, 128)
    part = jnp.sum(lax.all_to_all(flat, FINE, 0, 0, tiled=True), axis=0)
    total = lax.all_to_all(jnp.broadcast_to(part[None], (128, 4, 128)), FINE, 0, 0, tiled=True).reshape(-1)
    small_sums, at = [], 0
    for a in stacked:
        small_sums.append(total[at : at + a.size].reshape(a.shape))
        at += a.size

    both = lambda group, i, lo, hi: jnp.stack([large[l][group][i][:, lo:hi] for l in range(LAYERS)])
    return (
        output,
        input_grad,
        small_sums[0],
        small_sums[1],
        both("x", 0, 0, 256),
        both("z", 0, 0, 256),
        both("x", 0, 256, 768),
        both("z", 0, 256, 768),
        both("y", 0, 0, 512),
        small_sums[2],
        small_sums[3],
        small_sums[4],
        small_sums[5],
        both("x", 1, 0, 1408),
        both("z", 1, 0, 1408),
        both("y", 1, 0, 1408),
    )


def solution(mesh):
    fine = Mesh(mesh.devices.reshape(2, 4, 4, 2, 2), FINE)
    dp = ("yl", "x", "z", "c")
    every = P(FINE, None)
    mat = P(None, dp, "yh")
    rep = P()
    in_specs = (every, P(dp, None), every, rep, rep) + (mat,) * 5 + (rep,) * 4 + (mat,) * 3
    out_specs = (every, every, rep, rep) + (mat,) * 5 + (rep,) * 4 + (mat,) * 3
    return jax.shard_map(local, mesh=fine, in_specs=in_specs, out_specs=out_specs, check_vma=False)
```

```python
from functools import partial

import jax
import jax.numpy as jnp
from jax import lax
from jax.experimental import pallas as pl
from jax.experimental.pallas import tpu as pltpu
from jax.sharding import Mesh, PartitionSpec as P

LAYERS = 2
HEADS = 4
SPAN = 64
ATT = 2048
FF = 1408
ROWS = 256
D = 1024
KD = 128
VD = 256
FINE = ("yl", "x", "z", "c", "yh")
CHIPS = ("yh", "yl", "x", "z")
bf = jnp.bfloat16
f32 = jnp.float32
highest = lax.Precision.HIGHEST
norm_eps = 1e-06
group_eps = 1.0
decay_norm = 16.0
scale = KD**-0.5
NN = (((1,), (0,)), ((), ()))
NT = (((1,), (1,)), ((), ()))
TN = (((0,), (0,)), ((), ()))


def dot(a, b, dims=NN, precision=None):
    return lax.dot_general(a, b, dims, precision=precision, preferred_element_type=f32)


def call(kernel, out_shape, *, flops=0, moved=0, vmem=48, **kw):
    return pl.pallas_call(
        kernel,
        out_shape=out_shape,
        compiler_params=pltpu.CompilerParams(vmem_limit_bytes=vmem << 20),
        cost_estimate=pl.CostEstimate(flops=0, bytes_accessed=0, transcendentals=0),
        **kw,
    )


def shape(*dims, dtype=f32):
    return jax.ShapeDtypeStruct(dims, dtype)


def swap(a):
    return lax.ppermute(a, "c", [(0, 1), (1, 0)])


def ring(a, axis):
    if axis == "y":
        names = ("yl", "c", "yh")
        place = lambda i, c: ((i % 2) * 2 + c) * 2 + i // 2
    else:
        names = (axis, "c")
        place = lambda i, c: i * 2 + c
    pairs = [
        (place(i, c), place((i + 1 - 2 * c) % 4, c)) for i in range(4) for c in range(2)
    ]
    return lax.ppermute(a, names, pairs)


def shift(a, axis, step):
    if axis == "y":
        place = lambda i: (i % 2) * 2 + i // 2
        return lax.ppermute(a, ("yl", "yh"), [(place(i), place((i + step) % 4)) for i in range(4)])
    return lax.ppermute(a, axis, [(i, (i + step) % 4) for i in range(4)])


def chip_gather(s):
    return lax.all_gather(s, CHIPS, axis=0, tiled=True).reshape(2, 512, s.shape[1])


def after(value, *others):
    return lax.optimization_barrier((value, others))[0]


def add_kernel(plan, *refs):
    at = sum(count for _, count, _, _ in plan)
    outs, place = refs[at:], 0
    for out, count, start, n in plan:
        value = sum(t[...].reshape(t.shape[-2:]).astype(f32) for t in refs[place : place + count])
        outs[out][:, start : start + n] = value.astype(bf)
        place += count


def add_each(*groups):
    args, specs, outs, out_specs, plan, moved = [], [], [], [], [], 0
    for group in groups:
        start = 0
        for terms in group:
            for term in terms:
                a, which = term if isinstance(term, tuple) else (term, None)
                n = a.shape[-1]
                if which is None:
                    args.append(a.reshape(256, n))
                    specs.append(pl.BlockSpec((64, n), lambda i: (i, 0)))
                else:
                    args.append(a.reshape(2, 256, n))
                    specs.append(pl.BlockSpec((1, 64, n), lambda i, which=which: (which, i, 0)))
            plan.append((len(outs), len(terms), start, n))
            start += n
            moved += 512 * n * (len(terms) + 1)
        outs.append(shape(256, start, dtype=bf))
        out_specs.append(pl.BlockSpec((64, start), lambda i: (i, 0)))
    return call(
        partial(add_kernel, plan), tuple(outs), grid=(4,), in_specs=specs, out_specs=out_specs, flops=moved, moved=moved
    )(*args)


def split_kernel(plan, rows, extra, me, *refs):
    i = pl.program_id(0)
    at = sum(count for _, count, _, _ in plan) + extra
    outs, place = refs[at:], extra
    added = sum(t[...].astype(f32) for t in refs[:extra]).astype(bf)
    for group, count, start, n in plan:
        value = sum(t[...].reshape(t.shape[-2:]).astype(f32) for t in refs[place : place + count]).astype(bf)
        place += count
        for j in range(4):

            @pl.when(i == j)
            def _(out=outs[4 * group + j], value=value, start=start, n=n, group=group):
                out[:rows, start : start + n] = value
                if group == 0:
                    out[rows:, start : start + n] = added[:, start : start + n]


def split_sums(me, rows, groups, extra, extra_place):
    args, specs, outs, out_specs, plan = [], [], [], [], []
    for a in extra:
        args.append(a)
        specs.append(pl.BlockSpec((32, a.shape[1]), lambda i, me: (extra_place, 0)))
    for g, group in enumerate(groups):
        start = 0
        for terms in group:
            for term in terms:
                a, which = term if isinstance(term, tuple) else (term, None)
                n = a.shape[-1]
                if which is None:
                    args.append(a.reshape(-1, n))
                    specs.append(pl.BlockSpec((rows, n), lambda i, me, g=g: ((me[g] + i) % 4, 0)))
                else:
                    args.append(a.reshape(2, 4 * rows, n))
                    specs.append(pl.BlockSpec((1, rows, n), lambda i, me, g=g, which=which: (which, (me[g] + i) % 4, 0)))
            plan.append((g, len(terms), start, n))
            start += n
        dims = (rows + (32 if g == 0 else 0), start)
        outs += [shape(*dims, dtype=bf)] * 4
        out_specs += [pl.BlockSpec(dims, lambda i, me: (0, 0))] * 4
    out = call(
        partial(split_kernel, plan, rows, len(extra)),
        tuple(outs),
        grid_spec=pltpu.PrefetchScalarGridSpec(num_scalar_prefetch=1, grid=(4,), in_specs=specs, out_specs=out_specs),
    )(me, *args)
    return [out[4 * g : 4 * g + 4] for g in range(len(groups))]


def sum_kernel(*refs):
    for g in range(len(refs) // 5):
        refs[4 * (len(refs) // 5) + g][...] = sum(t[...].astype(f32) for t in refs[4 * g : 4 * g + 4])


def sums_of(groups):
    return call(sum_kernel, tuple(shape(*g[0].shape) for g in groups))(*(a for g in groups for a in g))


def passed_on(blocks, axis):
    return [blocks[0]] + [shift(blocks[j], axis, j) for j in (1, 2, 3)]


class Order:
    def __init__(self):
        self.seen = ()

    def __call__(self, kernel, first, *rest):
        out = kernel(after(first, *self.seen), *rest)
        self.seen = (out,)
        return out


def sixteens(a):
    return a.reshape(16, 16, a.shape[-1])


def whole(*dims):
    return pl.BlockSpec(dims, lambda h: (0,) * len(dims))


def per_half(*dims):
    return pl.BlockSpec((1, *dims), lambda h: (h,) + (0,) * len(dims))


def weight(width, place):
    return [pl.BlockSpec((1, 512, width), lambda h: (h, 0, place))] * 2


def rms(v, gain):
    return v * lax.rsqrt(jnp.mean(v * v, axis=-1, keepdims=True) + norm_eps) * gain


def norm_back(v, gain, d_out):
    r = lax.rsqrt(jnp.mean(v * v, axis=-1, keepdims=True) + norm_eps)
    u = d_out * gain
    d_v = r * u - v * (r * r * r) * jnp.mean(u * v, axis=-1, keepdims=True)
    return d_v, jnp.sum(d_out * v * r, axis=0, keepdims=True)


def to_given_order(value, order):
    high = value.astype(bf)
    rest = value - high.astype(f32)
    mid = rest.astype(bf)
    low = (rest - mid.astype(f32)).astype(bf)
    return dot(high, order) + dot(mid, order) + dot(low, order)


def entry_kernel(hidden, cot, valid, order, gain, x_out, g_out, hn_out):
    x = dot(hidden[...], order[...], NT)
    x_out[...] = x
    g_out[...] = dot(cot[...], order[...], NT) * valid[...]
    hn_out[...] = rms(x, gain[...]).astype(bf)


def entry(hidden, cot, valid, order, gain):
    return call(
        entry_kernel,
        (shape(ROWS, D), shape(ROWS, D), shape(ROWS, D, dtype=bf)),
        flops=4 * ROWS * D * D,
        moved=8 * D * D,
    )(hidden, cot, valid, order, gain)


def proj_kernel(hn, low_down, low_up, bias, w, wt, out, latent_out, logits_out):
    out[0] = (dot(hn[:, :512], w[0]) + dot(hn[:, 512:], wt[0])).astype(bf)

    @pl.when(pl.program_id(0) == 0)
    def _():
        latent = dot(hn[...], low_down[...])
        latent_out[...] = latent
        logits_out[...] = dot(latent, low_up[...], NN, highest) + bias[...]


def proj(hn, low_down, low_up, bias, w, place):
    return call(
        proj_kernel,
        (shape(2, ROWS, 1536, dtype=bf), shape(ROWS, 16), shape(ROWS, 512)),
        grid=(2,),
        in_specs=[whole(ROWS, D), whole(D, 16), whole(16, 512), whole(1, 512)] + weight(1536, place),
        out_specs=[per_half(ROWS, 1536), whole(ROWS, 16), whole(ROWS, 512)],
        flops=4 * ROWS * D * 1536,
        moved=4 * D * 1536,
    )(hn, low_down, low_up, bias, *w)


def ffn_kernel(hm, x, gain, w, wt, pre_out, acted_out, x_out, hn_out, acc):
    h = pl.program_id(0)
    near, far = hm[:, :512], hm[:, 512:]
    gate = dot(near, w[0, :, :FF]) + dot(far, wt[0, :, :FF])
    up = dot(near, w[0, :, FF : 2 * FF]) + dot(far, wt[0, :, FF : 2 * FF])
    pre_out[0, :, :FF] = gate.astype(bf)
    pre_out[0, :, FF:] = up.astype(bf)
    acted = (gate * jax.nn.sigmoid(gate) * up).astype(bf)
    acted_out[0] = acted
    part = jnp.concatenate([dot(acted, w[0, :, 2 * FF :], NT), dot(acted, wt[0, :, 2 * FF :], NT)], axis=1)

    @pl.when(h == 0)
    def _():
        acc[...] = part

    @pl.when(h == 1)
    def _():
        total = x[...] + (acc[...] + part)
        x_out[...] = total
        hn_out[...] = rms(total, gain[...]).astype(bf)


def ffn(hm, x, gain, w, place):
    return call(
        ffn_kernel,
        (
            shape(2, ROWS, 2 * FF, dtype=bf),
            shape(2, ROWS, FF, dtype=bf),
            shape(ROWS, D),
            shape(ROWS, D, dtype=bf),
        ),
        grid=(2,),
        in_specs=[whole(ROWS, D), whole(ROWS, D), whole(1, D)] + weight(3 * FF, place),
        out_specs=[per_half(ROWS, 2 * FF), per_half(ROWS, FF), whole(ROWS, D), whole(ROWS, D)],
        scratch_shapes=[pltpu.VMEM((ROWS, D), f32)],
        flops=12 * ROWS * D * FF,
        moved=12 * D * FF,
    )(hm, x, gain, *w)


def ffn_both_kernel(
    hm, x, order, g, gain, w, wt, acted_out, d_out, x_out, gb_out, g_out, gm_out, gain_out, acc, acc_back
):
    h = pl.program_id(0)
    near, far = hm[:, :512], hm[:, 512:]
    gate = dot(near, w[0, :, :FF]) + dot(far, wt[0, :, :FF])
    up = dot(near, w[0, :, FF : 2 * FF]) + dot(far, wt[0, :, FF : 2 * FF])
    sg = jax.nn.sigmoid(gate)
    acted = (gate * sg * up).astype(bf)
    acted_out[0] = acted
    part = jnp.concatenate([dot(acted, w[0, :, 2 * FF :], NT), dot(acted, wt[0, :, 2 * FF :], NT)], axis=1)
    gb = g[...].astype(bf)
    da = dot(gb[:, :512], w[0, :, 2 * FF :]) + dot(gb[:, 512:], wt[0, :, 2 * FF :])
    d_gate = (da * up * sg * (1.0 + gate * (1.0 - sg))).astype(bf)
    d_up = (da * gate * sg).astype(bf)
    d_out[0, :, :FF] = d_gate
    d_out[0, :, FF:] = d_up
    back = jnp.concatenate(
        [dot(d_gate, v[0, :, :FF], NT) + dot(d_up, v[0, :, FF : 2 * FF], NT) for v in (w, wt)], axis=1
    )

    @pl.when(h == 0)
    def _():
        acc[...] = part
        acc_back[...] = back
        gb_out[...] = gb

    @pl.when(h == 1)
    def _():
        x_out[...] = to_given_order(x[...] + (acc[...] + part), order[...])
        d_v, d_gain = norm_back(x[...], gain[...], acc_back[...] + back)
        total = g[...] + d_v
        g_out[...] = total
        gm_out[...] = total.astype(bf)
        gain_out[...] = d_gain


def ffn_both(hm, x, order, g, gain, w, place):
    return call(
        ffn_both_kernel,
        (
            shape(2, ROWS, FF, dtype=bf),
            shape(2, ROWS, 2 * FF, dtype=bf),
            shape(ROWS, D),
            shape(ROWS, D, dtype=bf),
            shape(ROWS, D),
            shape(ROWS, D, dtype=bf),
            shape(1, D),
        ),
        grid=(2,),
        in_specs=[whole(ROWS, D), whole(ROWS, D), whole(D, D), whole(ROWS, D), whole(1, D)] + weight(3 * FF, place),
        out_specs=[
            per_half(ROWS, FF), per_half(ROWS, 2 * FF), whole(ROWS, D), whole(ROWS, D), whole(ROWS, D),
            whole(ROWS, D), whole(1, D),
        ],
        scratch_shapes=[pltpu.VMEM((ROWS, D), f32)] * 2,
        flops=24 * ROWS * D * FF,
        moved=12 * D * FF,
    )(hm, x, order, g, gain, *w)


def ffn_back_kernel(g, x, gain, pre, w, wt, d_out, gb_out, g_out, gm_out, gain_out, acc):
    h = pl.program_id(0)
    gb = g[...].astype(bf)
    da = dot(gb[:, :512], w[0, :, 2 * FF :]) + dot(gb[:, 512:], wt[0, :, 2 * FF :])
    gate = pre[0, :, :FF].astype(f32)
    up = pre[0, :, FF:].astype(f32)
    sg = jax.nn.sigmoid(gate)
    d_gate = (da * up * sg * (1.0 + gate * (1.0 - sg))).astype(bf)
    d_up = (da * gate * sg).astype(bf)
    d_out[0, :, :FF] = d_gate
    d_out[0, :, FF:] = d_up
    part = jnp.concatenate(
        [
            dot(d_gate, v[0, :, :FF], NT) + dot(d_up, v[0, :, FF : 2 * FF], NT)
            for v in (w, wt)
        ],
        axis=1,
    )

    @pl.when(h == 0)
    def _():
        acc[...] = part
        gb_out[...] = gb

    @pl.when(h == 1)
    def _():
        d_v, d_gain = norm_back(x[...], gain[...], acc[...] + part)
        total = g[...] + d_v
        g_out[...] = total
        gm_out[...] = total.astype(bf)
        gain_out[...] = d_gain


def ffn_back(g, x, gain, pre, w, place):
    return call(
        ffn_back_kernel,
        (
            shape(2, ROWS, 2 * FF, dtype=bf),
            shape(ROWS, D, dtype=bf),
            shape(ROWS, D),
            shape(ROWS, D, dtype=bf),
            shape(1, D),
        ),
        grid=(2,),
        in_specs=[whole(ROWS, D), whole(ROWS, D), whole(1, D), per_half(ROWS, 2 * FF)] + weight(3 * FF, place),
        out_specs=[per_half(ROWS, 2 * FF), whole(ROWS, D), whole(ROWS, D), whole(ROWS, D), whole(1, D)],
        scratch_shapes=[pltpu.VMEM((ROWS, D), f32)],
        flops=12 * ROWS * D * FF,
        moved=12 * D * FF,
    )(g, x, gain, pre, *w)


def attn_back_kernel(first, d, d_logits, x, gain, g, low_up, low_down, order, w, wt, g_out, gain_out, latent_out, acc):
    h = pl.program_id(0)
    part = jnp.concatenate([dot(d[0], w[0], NT), dot(d[0], wt[0], NT)], axis=1)

    @pl.when(h == 0)
    def _():
        acc[...] = part

    @pl.when(h == 1)
    def _():
        d_latent = dot(d_logits[...], low_up[...], NT, highest)
        latent_out[...] = d_latent
        d_hn = acc[...] + part + dot(d_latent, low_down[...], NT, highest)
        d_v, d_gain = norm_back(x[...], gain[...], d_hn)
        total = g[...] + d_v
        g_out[...] = to_given_order(total, order[...]) if first else total
        gain_out[...] = d_gain


def attn_back(d, d_logits, x, gain, g, low_up, low_down, order, w, place, first):
    return call(
        partial(attn_back_kernel, first),
        (shape(ROWS, D), shape(1, D), shape(ROWS, 16)),
        grid=(2,),
        in_specs=[
            per_half(ROWS, 1536), whole(ROWS, 512), whole(ROWS, D), whole(1, D), whole(ROWS, D),
            whole(16, 512), whole(D, 16), whole(*order.shape),
        ]
        + weight(1536, place),
        out_specs=[whole(ROWS, D), whole(1, D), whole(ROWS, 16)],
        scratch_shapes=[pltpu.VMEM((ROWS, D), f32)],
        flops=4 * ROWS * D * 1536,
        moved=4 * D * 1536,
    )(d, d_logits, x, gain, g, low_up, low_down, order, *w)


def select_kernel(a, sel, out):
    out[0] = dot(a[...], sel[0], NT).astype(bf)


def select(a, sel):
    n = sel.shape[1]
    both = call(
        select_kernel,
        shape(2, ROWS, n, dtype=bf),
        grid=(2,),
        in_specs=[whole(ROWS, D), per_half(n, D)],
        out_specs=per_half(ROWS, n),
        flops=4 * ROWS * D * n,
        moved=4 * D * n,
    )(a, sel)
    return both, swap(both)


def own_weight_kernel(a, ar, b, br, d, dr, e, er, out):
    n = d.shape[-1]
    out[0, :, :n] = (dot(a[...], d[0], TN) + dot(ar[...], dr[0], TN)).astype(bf)
    out[0, :, n:] = (dot(b[...], e[0], TN) + dot(br[...], er[0], TN)).astype(bf)


def own_weight(a, ar, d, dr, b, br, e, er):
    n, m = d.shape[-1], e.shape[-1]
    near, far = pl.BlockSpec((ROWS, 512), lambda h: (0, 0)), pl.BlockSpec((ROWS, 512), lambda h: (0, 1))
    return call(
        own_weight_kernel,
        shape(2, 512, n + m, dtype=bf),
        grid=(2,),
        in_specs=[near, far] * 2 + [per_half(ROWS, n)] * 2 + [per_half(ROWS, m)] * 2,
        out_specs=per_half(512, n + m),
    )(a, ar, b, br, d, dr, e, er)


def x_weight_kernel(sets, lead, *refs):
    u, u1, u0 = refs[-3:]
    at = 0
    for i in range(sets):
        a, ar, d, dr = refs[4 * i : 4 * i + 4]
        n = d.shape[-1]
        r = (dot(a[0], d[0], TN) + dot(ar[0], dr[0], TN)).astype(bf)
        to = slice(at, at + n)
        part = lambda i: r[i * 128 : (i + 1) * 128].reshape(lead, 128 // lead, n)
        u[0, :, 0, :, to] = part(0)
        u[1, :, 0, :, to] = part(1)
        u1[:, 0, :, to] = part(2)
        u0[:, 0, :, to] = part(3)
        at += n


def x_weight(group, *sets):
    lead = (4, 1)[group]
    total, args, specs = 0, [], []
    for (a, ar), d, dr in sets:
        n = d.shape[-1] // 2
        args += [a, ar, d, dr]
        specs += [
            pl.BlockSpec((1, ROWS, 512), lambda h: (0, 0, group)),
            pl.BlockSpec((1, ROWS, 512), lambda h: (1, 0, group)),
        ]
        specs += [pl.BlockSpec((1, ROWS, n), lambda h: (h, 0, group))] * 2
        total += n
    dims = (lead, 2, 128 // lead, total)
    return call(
        partial(x_weight_kernel, len(sets), lead),
        (shape(2, *dims, dtype=bf), shape(*dims, dtype=bf), shape(*dims, dtype=bf)),
        grid=(2,),
        in_specs=specs,
        out_specs=[pl.BlockSpec((2, lead, 1, 128 // lead, total), lambda h: (0, 0, h, 0, 0))]
        + [pl.BlockSpec((lead, 1, 128 // lead, total), lambda h: (0, h, 0, 0))] * 2,
        flops=4 * ROWS * D * total,
        moved=2 * D * total,
    )(*args)


def y_weight_kernel(sets, where_, *refs):
    u, u1, u0 = refs[-3:]
    h, h2 = where_[0], where_[1]
    at = 0
    for i in range(sets):
        a, ar, d, dr = refs[4 * i : 4 * i + 4]
        n = d.shape[-1]
        to = slice(at, at + n)
        near = lambda place: dot(a[0, :, :256], d[place], TN) + dot(ar[1, :, :256], dr[place], TN)
        u0[:, to] = near(h).astype(bf)
        u[0, :, to] = near(1 - h).astype(bf)
        r = (dot(a[0, :, 256:], d[h2], TN) + dot(ar[1, :, 256:], dr[h2], TN)).astype(bf)
        u1[:, to] = r[:256]
        u[1, :, to] = r[256:]
        at += n


def y_weight(where_, *sets):
    total = sum(d.shape[-1] for _, d, _ in sets)
    args = [v for (a, ar), d, dr in sets for v in (a, ar, d, dr)]
    vm = pl.BlockSpec(memory_space=pltpu.VMEM)
    return call(
        partial(y_weight_kernel, len(sets)),
        (shape(2, 256, total, dtype=bf), shape(256, total, dtype=bf), shape(256, total, dtype=bf)),
        in_specs=[pl.BlockSpec(memory_space=pltpu.SMEM)] + [vm] * len(args),
        out_specs=(vm,) * 3,
        flops=4 * ROWS * D * total,
        moved=2 * D * total,
    )(where_, *args)


def log_sigmoid(v):
    return jnp.minimum(v, 0.0) - jnp.log1p(jnp.exp(-jnp.abs(v)))


def decays(logits):
    ld = log_sigmoid(logits) / decay_norm
    r = lax.broadcasted_iota(jnp.int32, (ROWS, ROWS), 0)
    c = lax.broadcasted_iota(jnp.int32, (ROWS, ROWS), 1)
    lower = ((r >= c) & (r // SPAN == c // SPAN)).astype(f32)
    cum = dot(lower, ld, NN, highest)
    blocks = [cum[i * SPAN : (i + 1) * SPAN] for i in range(4)]
    ends = [b[SPAN - 1 :] for b in blocks]
    return blocks, ends


def run_sum(ends, start, stop):
    total = jnp.zeros_like(ends[0])
    for i in range(start, stop):
        total = total + ends[i]
    return total


def key_factors(blocks, ends, i):
    parts = [jnp.exp((ends[j] - blocks[j]) + run_sum(ends, j + 1, i)) for j in range(i)]
    parts.append(jnp.exp(-blocks[i]))
    return jnp.concatenate(parts, axis=0)


def allowed(segr, segc, i):
    rows_i = segr[i * SPAN : (i + 1) * SPAN]
    count = (i + 1) * SPAN
    r = lax.broadcasted_iota(jnp.int32, (SPAN, count), 0) + i * SPAN
    c = lax.broadcasted_iota(jnp.int32, (SPAN, count), 1)
    return (r >= c) & (rows_i == segc[:, :count])


def start_factors(blocks, ends):
    return jnp.concatenate([jnp.exp(blocks[i] + run_sum(ends, 0, i)) for i in range(4)], axis=0)


def tail_factors(blocks, ends):
    return jnp.concatenate([jnp.exp((ends[i] - blocks[i]) + run_sum(ends, i + 1, 4)) for i in range(4)], axis=0)


def state_kernel(k, v, logits, segr, state):
    blocks, ends = decays(logits[...])
    segr = segr[...]
    tail_k = jnp.where(segr == segr[ROWS - 1 :], k[0].astype(f32) * tail_factors(blocks, ends), 0.0).astype(bf)
    state[0] = dot(tail_k, v[0], TN).astype(bf)


def mix_kernel(q, k, v, logits, segr, segc, out, state_q):
    blocks, ends = decays(logits[...])
    kf = k[0].astype(f32)
    qf = q[0].astype(f32) * scale
    segr, segc = segr[...], segc[...]
    state_q[0] = jnp.where(segr == segr[:1], qf * start_factors(blocks, ends), 0.0).astype(bf)
    for i in range(4):
        count = (i + 1) * SPAN
        qe = (qf[i * SPAN : count] * jnp.exp(blocks[i])).astype(bf)
        ke = (kf[:count] * key_factors(blocks, ends, i)).astype(bf)
        p = jnp.where(allowed(segr, segc, i), dot(qe, ke, NT), 0.0).astype(bf)
        out[0, i * SPAN : count] = dot(p, v[0, :count])


def head_cols(width, first=0):
    return pl.BlockSpec((1, ROWS, width), lambda t: (t // 2, 0, first + t % 2))


def by_head(*dims):
    return pl.BlockSpec((1, *dims), lambda t: (t,) + (0,) * len(dims))


def end_state(qkvg, logits, segr):
    return call(
        state_kernel,
        shape(HEADS, KD, VD, dtype=bf),
        grid=(HEADS,),
        in_specs=[head_cols(KD, 6), head_cols(VD, 1), pl.BlockSpec((ROWS, KD), lambda t: (0, t)), whole(ROWS, 1)],
        out_specs=by_head(KD, VD),
        flops=HEADS * 20_000_000,
        moved=2_000_000,
    )(qkvg, qkvg, logits, segr)


def mix(qkvg, logits, segr, segc):
    return call(
        mix_kernel,
        (shape(2, ROWS, 2 * VD), shape(HEADS, ROWS, KD, dtype=bf)),
        grid=(HEADS,),
        in_specs=[
            head_cols(KD),
            head_cols(KD, 6),
            head_cols(VD, 1),
            pl.BlockSpec((ROWS, KD), lambda t: (0, t)),
            whole(ROWS, 1),
            whole(1, ROWS),
        ],
        out_specs=[head_cols(VD), by_head(ROWS, KD)],
        flops=HEADS * 120_000_000,
        moved=4_000_000,
    )(qkvg, qkvg, qkvg, logits, segr, segc)


def out_weight(place):
    return [pl.BlockSpec((1, 512, VD), lambda t: (t // 2, 0, place * 2 + t % 2))] * 2


def out_kernel(local, state_q, state, g, gain, x, norm_gain, w, wt, mixed_out, rows, x_out, hm_out, acc):
    t = pl.program_id(0)
    mixed = local[0] + dot(state_q[0], state[0])
    mixed_out[0] = mixed
    gate = g[0].astype(f32)
    on = mixed * lax.rsqrt(jnp.mean(mixed * mixed, axis=-1, keepdims=True) + group_eps) * gain[...]
    mine = (on * gate * jax.nn.sigmoid(gate)).astype(bf)
    rows[0] = mine
    part = jnp.concatenate([dot(mine, w[0], NT), dot(mine, wt[0], NT)], axis=1)

    @pl.when(t == 0)
    def _():
        acc[...] = x[...]

    acc[...] += part

    @pl.when(t == HEADS - 1)
    def _():
        total = acc[...]
        x_out[...] = total
        hm_out[...] = rms(total, norm_gain[...]).astype(bf)


def out_rows(local, state_q, state, qkvg, gain, x, norm_gain, w, place):
    return call(
        out_kernel,
        (
            shape(2, ROWS, 2 * VD),
            shape(2, ROWS, 2 * VD, dtype=bf),
            shape(ROWS, D),
            shape(ROWS, D, dtype=bf),
        ),
        grid=(HEADS,),
        in_specs=[
            head_cols(VD), by_head(ROWS, KD), by_head(KD, VD), head_cols(VD, 4), whole(1, VD),
            whole(ROWS, D), whole(1, D),
        ]
        + out_weight(place),
        out_specs=[head_cols(VD), head_cols(VD), whole(ROWS, D), whole(ROWS, D)],
        scratch_shapes=[pltpu.VMEM((ROWS, D), f32)],
        flops=2 * ROWS * D * D + HEADS * 20_000_000,
        moved=2 * D * D + 5_000_000,
    )(local, state_q, state, qkvg, gain, x, norm_gain, *w)


def out_back_kernel(gm, mixed_in, g, gain_in, state_q, w, wt, dg_out, dgain, do_out, d_state):
    dr = dot(gm[:, :512], w[0]) + dot(gm[:, 512:], wt[0])
    mixed = mixed_in[0]
    gate = g[0].astype(f32)
    gain = gain_in[...]
    rho = lax.rsqrt(jnp.mean(mixed * mixed, axis=-1, keepdims=True) + group_eps)
    ng = mixed * rho
    sg = jax.nn.sigmoid(gate)
    d_on = dr * gate * sg
    dg_out[0] = (dr * ng * gain * sg * (1.0 + gate * (1.0 - sg))).astype(bf)
    dgain[0] = jnp.sum(d_on * ng, axis=0, keepdims=True)
    w_ = d_on * gain
    do = (rho * (w_ - ng * jnp.mean(w_ * ng, axis=-1, keepdims=True))).astype(bf)
    do_out[0] = do
    d_state[0] = dot(state_q[0], do, TN).astype(bf)


def out_back(gm, mixed, qkvg, gain, state_q, w, place):
    return call(
        out_back_kernel,
        (
            shape(2, ROWS, 2 * VD, dtype=bf),
            shape(HEADS, 1, VD),
            shape(2, ROWS, 2 * VD, dtype=bf),
            shape(HEADS, KD, VD, dtype=bf),
        ),
        grid=(HEADS,),
        in_specs=[whole(ROWS, D), head_cols(VD), head_cols(VD, 4), whole(1, VD), by_head(ROWS, KD)] + out_weight(place),
        out_specs=[head_cols(VD), by_head(1, VD), head_cols(VD), by_head(KD, VD)],
        flops=2 * ROWS * D * D + HEADS * 20_000_000,
        moved=2 * D * D + 5_000_000,
    )(gm, mixed, qkvg, gain, state_q, *w)


def mix_back_kernel(
    do_in, q, k, v, logits, segr, segc, state_in, state_q_in, dq_out, dk_out, dv_out, net_out
):
    do = do_in[0]
    blocks, ends = decays(logits[...])
    kf = k[0].astype(f32)
    qf = q[0].astype(f32) * scale
    segr, segc = segr[...], segc[...]
    sq = state_q_in[0]
    from_state = dot(do, state_in[0], NT)
    start = jnp.where(segr == segr[:1], start_factors(blocks, ends), 0.0) * scale
    dq_state = from_state * start
    net_state = from_state * sq.astype(f32)
    dk = jnp.zeros((ROWS, KD), f32)
    dv = jnp.zeros((ROWS, VD), f32)
    net_k = jnp.zeros((ROWS, KD), f32)
    nets = []
    grow = lambda a: a if a.shape[0] == ROWS else jnp.concatenate(
        [a, jnp.zeros((ROWS - a.shape[0], a.shape[1]), f32)], axis=0
    )
    for i in range(4):
        count = (i + 1) * SPAN
        here = slice(i * SPAN, count)
        eb = jnp.exp(blocks[i])
        qe = (qf[here] * eb).astype(bf)
        factors = key_factors(blocks, ends, i)
        ke = (kf[:count] * factors).astype(bf)
        keep = allowed(segr, segc, i)
        p = jnp.where(keep, dot(qe, ke, NT), 0.0).astype(bf)
        dp = jnp.where(keep, dot(do[here], v[0, :count], NT), 0.0).astype(bf)
        dv = dv + grow(dot(p, do[here], TN))
        dqe = dot(dp, ke)
        dq_out[0, here] = (dqe * eb * scale + dq_state[here]).astype(bf)
        nets.append(dqe * qe.astype(f32) + net_state[here])
        dke = dot(dp, qe, TN)
        dk = dk + grow(dke * factors)
        net_k = net_k + grow(dke * ke.astype(f32))
    dk_out[0] = dk
    dv_out[0] = dv
    net_out[0] = jnp.concatenate(nets, axis=0) - net_k


def mix_back(do, qkvg, logits, segr, segc, state, state_q):
    return call(
        mix_back_kernel,
        (
            shape(2, ROWS, 2 * KD, dtype=bf),
            shape(HEADS, ROWS, KD),
            shape(HEADS, ROWS, VD),
            shape(HEADS, ROWS, KD),
        ),
        grid=(HEADS,),
        in_specs=[
            head_cols(VD),
            head_cols(KD),
            head_cols(KD, 6),
            head_cols(VD, 1),
            pl.BlockSpec((ROWS, KD), lambda t: (0, t)),
            whole(ROWS, 1),
            whole(1, ROWS),
            by_head(KD, VD),
            by_head(ROWS, KD),
        ],
        out_specs=[head_cols(KD), by_head(ROWS, KD), by_head(ROWS, VD), by_head(ROWS, KD)],
        flops=HEADS * 300_000_000,
        moved=8_000_000,
    )(do, qkvg, qkvg, qkvg, logits, segr, segc, state, state_q)


def decay_back_kernel(dk_in, dv_in, net, k, v, logits_in, segr, segc, d_state, dk_out, dv_out, d_logits):
    logits = logits_in[...]
    blocks, ends = decays(logits)
    segr, segc = segr[...], segc[...]
    kf = k[0].astype(f32)
    tail = jnp.where(segr == segr[ROWS - 1 :], tail_factors(blocks, ends), 0.0)
    tail_k = (kf * tail).astype(bf)
    ds = d_state[0]
    back = dot(v[0], ds, NT)
    dk_out[0] = (dk_in[0] + back * tail).astype(bf)
    dv_out[0] = (dv_in[0] + dot(tail_k, ds)).astype(bf)
    r = lax.broadcasted_iota(jnp.int32, (ROWS, ROWS), 0)
    c = lax.broadcasted_iota(jnp.int32, (ROWS, ROWS), 1)
    same = segr == segc
    after = jnp.where(same & (c >= r), 1.0, 0.0)
    before = jnp.where(same & (c < r), 1.0, 0.0)
    d_ld = dot(after, net[0], NN, highest) + dot(before, back * tail_k.astype(f32), NN, highest)
    d_logits[...] = d_ld * jax.nn.sigmoid(-logits) / decay_norm


def decay_back(dk, dv, net, qkvg, logits, segr, segc, d_state):
    return call(
        decay_back_kernel,
        (
            shape(2, ROWS, 2 * KD, dtype=bf),
            shape(2, ROWS, 2 * VD, dtype=bf),
            shape(ROWS, HEADS * KD),
        ),
        grid=(HEADS,),
        in_specs=[
            by_head(ROWS, KD),
            by_head(ROWS, VD),
            by_head(ROWS, KD),
            head_cols(KD, 6),
            head_cols(VD, 1),
            pl.BlockSpec((ROWS, KD), lambda t: (0, t)),
            whole(ROWS, 1),
            whole(1, ROWS),
            by_head(KD, VD),
        ],
        out_specs=[head_cols(KD), head_cols(VD), pl.BlockSpec((ROWS, KD), lambda t: (0, t))],
        flops=HEADS * 100_000_000,
        moved=4_000_000,
    )(dk, dv, net, qkvg, qkvg, logits, segr, segc, d_state)


def one_hot(places):
    return (places[:, None] == jnp.arange(D, dtype=jnp.int32)[None, :]).astype(bf)


def orders():
    yl, x, z, c, yh = (lax.axis_index(a) for a in FINE)
    k = jnp.arange(D, dtype=jnp.int32)
    base = one_hot((k % 512) // 16 * 32 + jnp.where(k < 512, c, 1 - c) * 16 + k % 16)
    s = 1 - 2 * c
    pick = lambda table, b: jnp.sum(jnp.where(b[:, None] == jnp.arange(table.shape[0])[None], table[None], 0), axis=1)
    far = jnp.array([0, 1, 0, 0, 1, 0, 1, 1], jnp.int32)
    steps = lambda a: jnp.stack([a + 2, a + s, a + s, a, a + 2, a - s, a - s, a]) % 4
    block, r = k // 128, k % 128
    rr = r % 16
    index = lambda far, yl, x, z: far * 512 + ((yl * 4 + x) * 4 + z) * 16 + rr
    along_x = index(pick(far, block), (r // 16) % 2, pick(steps(x), block), r // 32)
    along_z = index(pick(far, block), r // 64, (r // 16) % 4, pick(steps(z), block))
    k = jnp.arange(1536, dtype=jnp.int32)
    block, r = k // 256, k % 256
    rr = r % 16
    along_y = index(
        pick(jnp.array([0, 0, 1, 1, 1, 0], jnp.int32), block),
        pick(jnp.stack([yl, 1 - yl, 1 - yl, yl, 1 - yl, 1 - yl]), block),
        r // 64,
        (r // 16) % 4,
    )
    next_half = ((yh * 2 + yl + s) % 4) // 2
    along_x, along_z, along_y = (a.reshape(2, -1) for a in (along_x, along_z, along_y))
    sel_xz = one_hot(jnp.concatenate([along_x, along_z], axis=1).reshape(-1)).reshape(2, D, D)
    sel_y = one_hot(along_y.reshape(-1)).reshape(2, 768, D)
    return base, sel_xz, sel_y, jnp.stack([yh, next_half]).astype(jnp.int32), jnp.stack([z, yh * 2 + yl, x, yh * 2 + yl, x, z]).astype(jnp.int32)


def own_first(a, axis):
    shape_ = a.shape
    a = a.reshape(*shape_[:axis], 32, 2, 16, *shape_[axis + 1 :])
    zero, one = (lax.index_in_dim(a, i, axis + 1, keepdims=False).reshape(*shape_[:axis], 512, *shape_[axis + 1 :]) for i in (0, 1))
    first = lax.axis_index("c") == 0
    return jnp.concatenate([jnp.where(first, zero, one), jnp.where(first, one, zero)], axis=axis)


def given_order(a, axis):
    shape_ = a.shape
    near, far = lax.slice_in_dim(a, 0, 512, axis=axis), lax.slice_in_dim(a, 512, 1024, axis=axis)
    first = lax.axis_index("c") == 0
    blocks = [b.reshape(*shape_[:axis], 32, 16, *shape_[axis + 1 :]) for b in (jnp.where(first, near, far), jnp.where(first, far, near))]
    return jnp.stack(blocks, axis=axis + 1).reshape(shape_)


def local(
    hidden_in, lengths, cotangent, norm_in, norm_mid, query_w, key_w, value_w, gate_w, out_w,
    low_down, low_up, decay_bias, group_gain, ffn_gate, ffn_up, ffn_down,
):
    yh = lax.axis_index("yh")
    qkvg = [(query_w[l], value_w[l], key_w[l], gate_w[l]) for l in range(LAYERS)]
    feeds = [(ffn_gate[l], ffn_up[l], ffn_down[l]) for l in range(LAYERS)]
    pad = jnp.zeros((16, 128), bf)
    gathered = chip_gather(jnp.concatenate([*qkvg[0], *qkvg[1], out_w[0], out_w[1], pad, *feeds[0]], axis=1))
    gathered_late = chip_gather(jnp.concatenate(feeds[1], axis=1))
    gathered = (gathered, swap(gathered))
    attn_w = [(gathered, 0, 6), (gathered, 1, 7)]
    feed_w = [(gathered, 1), None]

    order, sel_xz, sel_y, where_, me = orders()
    bounds = jnp.cumsum(lengths[0])
    places = jnp.arange(ROWS, dtype=jnp.int32) + yh * ROWS
    seg = jnp.sum((places[:, None] >= bounds[None, :]).astype(jnp.int32), axis=1)
    valid = (seg < lengths.shape[1]).astype(f32)
    segr, segc = seg[:, None], seg[None, :]
    gains_in, gains_mid = own_first(norm_in, 1), own_first(norm_mid, 1)
    downs = own_first(low_down, 1)

    order = after(order, sel_xz, sel_y, segr, segc)
    x, g, hn = entry(hidden_in, cotangent, valid[:, None], order, gains_in[:1])
    saved = []
    for layer in range(LAYERS):
        w, at_qkvg, at_out = attn_w[layer]
        qkvg, latent, logits = proj(hn, downs[layer], low_up[layer], decay_bias[layer][None], w, at_qkvg)
        state = lax.ppermute(end_state(qkvg, logits, segr), "yh", [(0, 1)])
        local_mix, state_q = mix(qkvg, logits, segr, segc)
        mixed, rows, x_mid, hm = out_rows(
            local_mix, state_q, state, qkvg, group_gain[layer][None], x, gains_mid[layer : layer + 1], w, at_out
        )
        last = layer + 1 == LAYERS
        if last:
            gathered_late = after(gathered_late, local_mix)
            feed_w[1] = ((gathered_late, swap(gathered_late)), 0)
        if last:
            acted, d_pre, output, *back = ffn_both(hm, x_mid, order, g, gains_mid[layer : layer + 1], *feed_w[layer])
            saved.append((x, hn, qkvg, latent, logits, state, state_q, mixed, rows, x_mid, hm, None, acted))
        else:
            pre, acted, x_next, hn_next = ffn(hm, x_mid, gains_in[layer + 1 : layer + 2], *feed_w[layer])
            saved.append((x, hn, qkvg, latent, logits, state, state_q, mixed, rows, x_mid, hm, pre, acted))
            x, hn = x_next, hn_next

    def rings(u):
        return [ring(v[0].reshape(2, 16, 16, -1), a) for v, a in zip(u, "xzy")]

    def second_terms(u, r):
        return add_each(*([(v[1], (w, 0))] for v, w in zip(u, r)))

    def second_rings(t):
        return [ring(sixteens(v), a) for v, a in zip(t, "xzy")]

    def last_terms(*parts):
        return [[(u[i][2], r1[i], (swap(r[i]), 1)) for u, r, r1 in parts] for i in range(3)]

    def weights(sets):
        return [x_weight(0, *sets[0]), x_weight(1, *sets[1]), y_weight(where_, *sets[2])]

    def flatten(small):
        stacked = [jnp.stack([part[i] for part in small]) for i in range(6)]
        for i in range(3):
            stacked[i] = given_order(stacked[i], 1)
        flat = jnp.concatenate([a.reshape(-1) for a in stacked])
        return stacked, jnp.pad(flat, (0, 32 * 2944 - flat.shape[0])).reshape(32, 2944)

    then = Order()
    small = [None] * LAYERS
    for layer in reversed(range(LAYERS)):
        x, hn, qkvg, latent, logits, state, state_q, mixed, rows, x_mid, hm, pre, acted = saved[layer]
        bottom = layer == 0
        w, at_qkvg, at_out = attn_w[layer]
        if bottom:
            d_pre, *back = then(ffn_back, g, x_mid, gains_mid[layer : layer + 1], pre, *feed_w[layer])
        gb, g_mid, gm, grad_mid = back
        d_pre_far, acted_far = swap(d_pre), swap(acted)
        d_g, d_gain, do, d_state = then(out_back, gm, mixed, qkvg, group_gain[layer][None], state_q, w, at_out)
        d_state = lax.ppermute(d_state, "yh", [(1, 0)])
        if bottom:
            hm_s, gb_s = then(select, hm, sel_xz), then(select, gb, sel_y)
            sets = (
                ((hm_s, d_pre, d_pre_far),),
                ((hm_s, d_pre, d_pre_far),),
                ((gb_s, acted, acted_far),),
            )
            sets = tuple(p + q for p, q in zip(attn_sets, sets))
            u = then(weights, sets)
            r = rings(u)
        else:
            t = then(own_weight, hm, swap(hm), d_pre, d_pre_far, gb, swap(gb), acted, acted_far)
            top = lax.psum_scatter(t.reshape(64, 16, 3 * FF), CHIPS, scatter_dimension=0, tiled=False)
        d_q, d_k, d_v, net = then(mix_back, do, qkvg, logits, segr, segc, state, state_q)
        d_k, d_v, d_logits = then(decay_back, d_k, d_v, net, qkvg, logits, segr, segc, d_state)
        d = jnp.concatenate([d_q, d_v, d_k, d_g], axis=2)
        d_far = swap(d)
        hn_s, gm_s = then(select, hn, sel_xz), then(select, gm, sel_y)
        attn_sets = (
            ((hn_s, d, d_far),),
            ((hn_s, d, d_far),),
            ((gm_s, rows, swap(rows)),),
        )
        if bottom:
            u_last = then(weights, attn_sets)
            r_last = rings(u_last)
            t1 = then(second_terms, u, r)
            r1 = second_rings(t1)
        g, grad_in, d_latent = then(
            attn_back,
            d, d_logits, x, gains_in[layer : layer + 1], g_mid, low_up[layer], downs[layer].astype(f32), order, w, at_qkvg, bottom
        )
        small[layer] = (
            grad_in[0],
            grad_mid[0],
            dot(hn.astype(f32), d_latent, TN, highest),
            dot(latent, d_logits, TN, highest),
            jnp.sum(d_logits, axis=0),
            jnp.sum(d_gain[:, 0], axis=0),
        )
        if bottom:
            stacked, flat = flatten(small)
            flat = flat + swap(flat)
            flat = flat.astype(bf)
            flat = [flat] + [shift(flat, "x", j) for j in (1, 2, 3)]
            t1_last = then(second_terms, u_last, after(r_last, flat[0]))
            r1_last = second_rings(t1_last)
    input_grad = g

    parts = last_terms((u, r, r1), (u_last, r_last, r1_last))
    parts = split_sums(me[:3], 64, parts, flat, 0)
    parts = [passed_on(p, a) for p, a in zip(parts, "zyx")]
    parts = split_sums(me[3:], 16, [[p] for p in parts], parts[0], 2)
    parts = [passed_on(p, a) for p, a in zip(parts, "yxz")]
    sums = dict(zip("xzy", sums_of(parts)))
    total = sums["x"][16:].reshape(-1)
    width = {"x": 768, "z": 768, "y": 512}
    small_sums, at = [], 0
    for a in stacked:
        small_sums.append(total[at : at + a.size].reshape(a.shape))
        at += a.size

    width = {"x": 768, "z": 768, "y": 512}

    def attn_part(group, lo, hi):
        at = FF + width[group]
        return jnp.stack([sums[group][:16, at + lo : at + hi], sums[group][:16, lo:hi]])

    def feed_part(group):
        at = width[group]
        place = "xzy".index(group) * FF
        return jnp.stack([sums[group][:16, at : at + FF], top[:, place : place + FF].astype(f32)])

    return (
        output,
        input_grad,
        small_sums[0],
        small_sums[1],
        attn_part("x", 0, 256),
        attn_part("z", 0, 256),
        attn_part("x", 256, 768),
        attn_part("z", 256, 768),
        attn_part("y", 0, 512),
        small_sums[2],
        small_sums[3],
        small_sums[4],
        small_sums[5],
        feed_part("x"),
        feed_part("z"),
        feed_part("y"),
    )


def solution(mesh):
    fine = Mesh(mesh.devices.reshape(2, 4, 4, 2, 2), FINE)
    dp = ("yl", "x", "z", "c")
    every = P(FINE, None)
    mat = P(None, dp, "yh")
    rep = P()
    in_specs = (every, P(dp, None), every, rep, rep) + (mat,) * 5 + (rep,) * 4 + (mat,) * 3
    out_specs = (every, every, rep, rep) + (mat,) * 5 + (rep,) * 4 + (mat,) * 3
    return jax.shard_map(local, mesh=fine, in_specs=in_specs, out_specs=out_specs, check_vma=False)
```

```python
from functools import partial

import jax
import jax.numpy as jnp
from jax import lax
from jax.experimental import pallas as pl
from jax.experimental.pallas import tpu as pltpu
from jax.sharding import Mesh, PartitionSpec as P

LAYERS = 2
HEADS = 4
SPAN = 64
ATT = 2048
FF = 1408
ROWS = 256
D = 1024
KD = 128
VD = 256
FINE = ("yl", "x", "z", "c", "yh")
CHIPS = ("yh", "yl", "x", "z")
bf = jnp.bfloat16
f32 = jnp.float32
highest = lax.Precision.HIGHEST
norm_eps = 1e-06
group_eps = 1.0
decay_norm = 16.0
scale = KD**-0.5
NN = (((1,), (0,)), ((), ()))
NT = (((1,), (1,)), ((), ()))
TN = (((0,), (0,)), ((), ()))


def dot(a, b, dims=NN, precision=None):
    return lax.dot_general(a, b, dims, precision=precision, preferred_element_type=f32)


def call(kernel, out_shape, *, flops=0, moved=0, vmem=48, **kw):
    return pl.pallas_call(
        kernel,
        out_shape=out_shape,
        compiler_params=pltpu.CompilerParams(vmem_limit_bytes=vmem << 20),
        cost_estimate=pl.CostEstimate(flops=flops or 500_000_000, bytes_accessed=moved or 8_000_000, transcendentals=0),
        **kw,
    )


def shape(*dims, dtype=f32):
    return jax.ShapeDtypeStruct(dims, dtype)


def swap(a):
    return lax.ppermute(a, "c", [(0, 1), (1, 0)])


def ring(a, axis):
    if axis == "y":
        names = ("yl", "c", "yh")
        place = lambda i, c: ((i % 2) * 2 + c) * 2 + i // 2
    else:
        names = (axis, "c")
        place = lambda i, c: i * 2 + c
    pairs = [
        (place(i, c), place((i + 1 - 2 * c) % 4, c)) for i in range(4) for c in range(2)
    ]
    return lax.ppermute(a, names, pairs)


def shift(a, axis, step):
    if axis == "y":
        place = lambda i: (i % 2) * 2 + i // 2
        return lax.ppermute(a, ("yl", "yh"), [(place(i), place((i + step) % 4)) for i in range(4)])
    return lax.ppermute(a, axis, [(i, (i + step) % 4) for i in range(4)])


def chip_gather(s):
    return lax.all_gather(s, CHIPS, axis=0, tiled=True).reshape(2, 512, s.shape[1])


def after(value, *others):
    return lax.optimization_barrier((value, others))[0]


def rows_part(t, start, n):
    v = t[...].reshape(t.shape[-2:])
    return (v if v.shape[1] == n else v[:, start : start + n]).astype(f32)


def add_kernel(plan, *refs):
    at = sum(count for _, count, _, _ in plan)
    outs, place = refs[at:], 0
    for out, count, start, n in plan:
        value = sum(rows_part(t, start, n) for t in refs[place : place + count])
        outs[out][:, start : start + n] = value.astype(bf)
        place += count


def add_each(*groups):
    args, specs, outs, out_specs, plan, moved = [], [], [], [], [], 0
    for group in groups:
        start = 0
        for terms in group:
            for term in terms:
                a, which = term if isinstance(term, tuple) else (term, None)
                wide = a.shape[-1]
                if which is None:
                    args.append(a.reshape(256, wide))
                    specs.append(pl.BlockSpec((64, wide), lambda i: (i, 0)))
                else:
                    args.append(a.reshape(2, 256, wide))
                    specs.append(pl.BlockSpec((1, 64, wide), lambda i, which=which: (which, i, 0)))
            n = terms[0].shape[-1]
            plan.append((len(outs), len(terms), start, n))
            start += n
            moved += 512 * n * (len(terms) + 1)
        outs.append(shape(256, start, dtype=bf))
        out_specs.append(pl.BlockSpec((64, start), lambda i: (i, 0)))
    return call(
        partial(add_kernel, plan), tuple(outs), grid=(4,), in_specs=specs, out_specs=out_specs, flops=moved, moved=moved
    )(*args)


def split_kernel(plan, rows, extra, me, *refs):
    i = pl.program_id(0)
    at = sum(count for _, count, _, _ in plan) + extra
    outs, place = refs[at:], extra
    added = sum(t[...].astype(f32) for t in refs[:extra]).astype(bf)
    for group, count, start, n in plan:
        value = sum(rows_part(t, start, n) for t in refs[place : place + count]).astype(bf)
        place += count
        for j in range(4):

            @pl.when(i == j)
            def _(out=outs[4 * group + j], value=value, start=start, n=n, group=group):
                out[:rows, start : start + n] = value
                if group == 0:
                    out[rows:, start : start + n] = added[:, start : start + n]


def split_sums(me, rows, groups, extra, extra_place):
    args, specs, outs, out_specs, plan = [], [], [], [], []
    for a in extra:
        args.append(a)
        specs.append(pl.BlockSpec((32, a.shape[1]), lambda i, me: (extra_place, 0)))
    for g, group in enumerate(groups):
        start = 0
        for terms in group:
            for term in terms:
                a, which = term if isinstance(term, tuple) else (term, None)
                wide = a.shape[-1]
                if which is None:
                    args.append(a.reshape(-1, wide))
                    specs.append(pl.BlockSpec((rows, wide), lambda i, me, g=g: ((me[g] + i) % 4, 0)))
                else:
                    args.append(a.reshape(2, 4 * rows, wide))
                    specs.append(pl.BlockSpec((1, rows, wide), lambda i, me, g=g, which=which: (which, (me[g] + i) % 4, 0)))
            n = terms[0].shape[-1]
            plan.append((g, len(terms), start, n))
            start += n
        dims = (rows + (32 if g == 0 else 0), start)
        outs += [shape(*dims, dtype=bf)] * 4
        out_specs += [pl.BlockSpec(dims, lambda i, me: (0, 0))] * 4
    out = call(
        partial(split_kernel, plan, rows, len(extra)),
        tuple(outs),
        grid_spec=pltpu.PrefetchScalarGridSpec(num_scalar_prefetch=1, grid=(4,), in_specs=specs, out_specs=out_specs),
    )(me, *args)
    return [out[4 * g : 4 * g + 4] for g in range(len(groups))]


def final_kernel(x, *refs):
    z, y, top = refs[:4], refs[4:8], refs[8]
    outs = refs[9:]
    groups = [sum(x[i].astype(f32) for i in range(16))]
    groups += [sum(t[...].astype(f32) for t in g) for g in (z, y)]
    outs[8][...] = groups[1][16:]
    for out, g, lo, hi in ((0, 0, 0, 256), (1, 1, 0, 256), (2, 0, 256, 768), (3, 1, 256, 768), (4, 2, 0, 512)):
        mine = groups[g].shape[1] - (512 if g == 2 else 768)
        outs[out][0] = groups[g][:16, mine + lo : mine + hi]
        outs[out][1] = groups[g][:16, lo:hi]
    for g in range(3):
        at = 512 if g == 2 else 768
        outs[5 + g][0] = groups[g][:16, at : at + FF]
        outs[5 + g][1] = top[:, g * FF : (g + 1) * FF].astype(f32)


def final_sums(x, z, y, top):
    widths = (256, 256, 512, 512, 512, FF, FF, FF)
    return call(final_kernel, tuple(shape(2, 16, w) for w in widths) + (shape(32, z[0].shape[1]),))(x, *z, *y, top)


def passed_on(blocks, axis):
    return [blocks[0]] + [shift(blocks[j], axis, j) for j in (1, 2, 3)]


class Order:
    def __init__(self):
        self.seen = ()

    def __call__(self, kernel, first, *rest):
        out = kernel(after(first, *self.seen), *rest)
        self.seen = (out,)
        return out


def sixteens(a):
    return a.reshape(16, 16, a.shape[-1])


def whole(*dims):
    return pl.BlockSpec(dims, lambda h: (0,) * len(dims))


def per_half(*dims):
    return pl.BlockSpec((1, *dims), lambda h: (h,) + (0,) * len(dims))


def weight(width, place, far_place=None):
    far_place = place if far_place is None else far_place
    return [pl.BlockSpec((1, 512, width), lambda h, p=p: (h, 0, p)) for p in (place, far_place)]


def rms(v, gain):
    return v * lax.rsqrt(jnp.mean(v * v, axis=-1, keepdims=True) + norm_eps) * gain


def norm_back(v, gain, d_out):
    r = lax.rsqrt(jnp.mean(v * v, axis=-1, keepdims=True) + norm_eps)
    u = d_out * gain
    d_v = r * u - v * (r * r * r) * jnp.mean(u * v, axis=-1, keepdims=True)
    return d_v, jnp.sum(d_out * v * r, axis=0, keepdims=True)


def to_given_order(value, order):
    high = value.astype(bf)
    rest = value - high.astype(f32)
    mid = rest.astype(bf)
    low = (rest - mid.astype(f32)).astype(bf)
    return dot(high, order) + dot(mid, order) + dot(low, order)


def entry_kernel(hidden, cot, valid, order, gain, x_out, g_out, hn_out):
    x = dot(hidden[...], order[...], NT)
    x_out[...] = x
    g_out[...] = dot(cot[...], order[...], NT) * valid[...]
    hn_out[...] = rms(x, gain[...]).astype(bf)


def entry(hidden, cot, valid, order, gain):
    return call(
        entry_kernel,
        (shape(ROWS, D), shape(ROWS, D), shape(ROWS, D, dtype=bf)),
        flops=4 * ROWS * D * D,
        moved=8 * D * D,
    )(hidden, cot, valid, order, gain)


def proj_kernel(hn, low_down, low_up, bias, w, wt, out, latent_out, logits_out):
    out[0] = (dot(hn[:, :512], w[0]) + dot(hn[:, 512:], wt[0])).astype(bf)

    @pl.when(pl.program_id(0) == 0)
    def _():
        latent = dot(hn[...], low_down[...])
        latent_out[...] = latent
        logits_out[...] = dot(latent, low_up[...], NN, highest) + bias[...]


def proj(hn, low_down, low_up, bias, w, place, far_place):
    return call(
        proj_kernel,
        (shape(2, ROWS, 1536, dtype=bf), shape(ROWS, 16), shape(ROWS, 512)),
        grid=(2,),
        in_specs=[whole(ROWS, D), whole(D, 16), whole(16, 512), whole(1, 512)] + weight(1536, place, far_place),
        out_specs=[per_half(ROWS, 1536), whole(ROWS, 16), whole(ROWS, 512)],
        flops=4 * ROWS * D * 1536,
        moved=4 * D * 1536,
    )(hn, low_down, low_up, bias, *w)


def ffn_kernel(hm, x, gain, w, wt, pre_out, acted_out, x_out, hn_out, acc):
    h = pl.program_id(0)
    near, far = hm[:, :512], hm[:, 512:]
    gate = dot(near, w[0, :, :FF]) + dot(far, wt[0, :, :FF])
    up = dot(near, w[0, :, FF : 2 * FF]) + dot(far, wt[0, :, FF : 2 * FF])
    pre_out[0, :, :FF] = gate.astype(bf)
    pre_out[0, :, FF:] = up.astype(bf)
    acted = (gate * jax.nn.sigmoid(gate) * up).astype(bf)
    acted_out[0] = acted
    part = jnp.concatenate([dot(acted, w[0, :, 2 * FF :], NT), dot(acted, wt[0, :, 2 * FF :], NT)], axis=1)

    @pl.when(h == 0)
    def _():
        acc[...] = part

    @pl.when(h == 1)
    def _():
        total = x[...] + (acc[...] + part)
        x_out[...] = total
        hn_out[...] = rms(total, gain[...]).astype(bf)


def ffn(hm, x, gain, w, place):
    return call(
        ffn_kernel,
        (
            shape(2, ROWS, 2 * FF, dtype=bf),
            shape(2, ROWS, FF, dtype=bf),
            shape(ROWS, D),
            shape(ROWS, D, dtype=bf),
        ),
        grid=(2,),
        in_specs=[whole(ROWS, D), whole(ROWS, D), whole(1, D)] + weight(3 * FF, place),
        out_specs=[per_half(ROWS, 2 * FF), per_half(ROWS, FF), whole(ROWS, D), whole(ROWS, D)],
        scratch_shapes=[pltpu.VMEM((ROWS, D), f32)],
        flops=12 * ROWS * D * FF,
        moved=12 * D * FF,
    )(hm, x, gain, *w)


def ffn_both_kernel(
    hm, x, order, g, gain, w, wt, acted_out, d_out, x_out, gb_out, g_out, gm_out, gain_out, acc, acc_back
):
    h = pl.program_id(0)
    near, far = hm[:, :512], hm[:, 512:]
    gate = dot(near, w[0, :, :FF]) + dot(far, wt[0, :, :FF])
    up = dot(near, w[0, :, FF : 2 * FF]) + dot(far, wt[0, :, FF : 2 * FF])
    sg = jax.nn.sigmoid(gate)
    acted = (gate * sg * up).astype(bf)
    acted_out[0] = acted
    part = jnp.concatenate([dot(acted, w[0, :, 2 * FF :], NT), dot(acted, wt[0, :, 2 * FF :], NT)], axis=1)
    gb = g[...].astype(bf)
    da = dot(gb[:, :512], w[0, :, 2 * FF :]) + dot(gb[:, 512:], wt[0, :, 2 * FF :])
    d_gate = (da * up * sg * (1.0 + gate * (1.0 - sg))).astype(bf)
    d_up = (da * gate * sg).astype(bf)
    d_out[0, :, :FF] = d_gate
    d_out[0, :, FF:] = d_up
    back = jnp.concatenate(
        [dot(d_gate, v[0, :, :FF], NT) + dot(d_up, v[0, :, FF : 2 * FF], NT) for v in (w, wt)], axis=1
    )

    @pl.when(h == 0)
    def _():
        acc[...] = part
        acc_back[...] = back
        gb_out[...] = gb

    @pl.when(h == 1)
    def _():
        x_out[...] = to_given_order(x[...] + (acc[...] + part), order[...])
        d_v, d_gain = norm_back(x[...], gain[...], acc_back[...] + back)
        total = g[...] + d_v
        g_out[...] = total
        gm_out[...] = total.astype(bf)
        gain_out[...] = d_gain


def ffn_both(hm, x, order, g, gain, w, place):
    return call(
        ffn_both_kernel,
        (
            shape(2, ROWS, FF, dtype=bf),
            shape(2, ROWS, 2 * FF, dtype=bf),
            shape(ROWS, D),
            shape(ROWS, D, dtype=bf),
            shape(ROWS, D),
            shape(ROWS, D, dtype=bf),
            shape(1, D),
        ),
        grid=(2,),
        in_specs=[whole(ROWS, D), whole(ROWS, D), whole(D, D), whole(ROWS, D), whole(1, D)] + weight(3 * FF, place),
        out_specs=[
            per_half(ROWS, FF), per_half(ROWS, 2 * FF), whole(ROWS, D), whole(ROWS, D), whole(ROWS, D),
            whole(ROWS, D), whole(1, D),
        ],
        scratch_shapes=[pltpu.VMEM((ROWS, D), f32)] * 2,
        flops=24 * ROWS * D * FF,
        moved=12 * D * FF,
    )(hm, x, order, g, gain, *w)


def ffn_back_kernel(g, x, gain, pre, w, wt, d_out, gb_out, g_out, gm_out, gain_out, acc):
    h = pl.program_id(0)
    gb = g[...].astype(bf)
    da = dot(gb[:, :512], w[0, :, 2 * FF :]) + dot(gb[:, 512:], wt[0, :, 2 * FF :])
    gate = pre[0, :, :FF].astype(f32)
    up = pre[0, :, FF:].astype(f32)
    sg = jax.nn.sigmoid(gate)
    d_gate = (da * up * sg * (1.0 + gate * (1.0 - sg))).astype(bf)
    d_up = (da * gate * sg).astype(bf)
    d_out[0, :, :FF] = d_gate
    d_out[0, :, FF:] = d_up
    part = jnp.concatenate(
        [
            dot(d_gate, v[0, :, :FF], NT) + dot(d_up, v[0, :, FF : 2 * FF], NT)
            for v in (w, wt)
        ],
        axis=1,
    )

    @pl.when(h == 0)
    def _():
        acc[...] = part
        gb_out[...] = gb

    @pl.when(h == 1)
    def _():
        d_v, d_gain = norm_back(x[...], gain[...], acc[...] + part)
        total = g[...] + d_v
        g_out[...] = total
        gm_out[...] = total.astype(bf)
        gain_out[...] = d_gain


def ffn_back(g, x, gain, pre, w, place):
    return call(
        ffn_back_kernel,
        (
            shape(2, ROWS, 2 * FF, dtype=bf),
            shape(ROWS, D, dtype=bf),
            shape(ROWS, D),
            shape(ROWS, D, dtype=bf),
            shape(1, D),
        ),
        grid=(2,),
        in_specs=[whole(ROWS, D), whole(ROWS, D), whole(1, D), per_half(ROWS, 2 * FF)] + weight(3 * FF, place),
        out_specs=[per_half(ROWS, 2 * FF), whole(ROWS, D), whole(ROWS, D), whole(ROWS, D), whole(1, D)],
        scratch_shapes=[pltpu.VMEM((ROWS, D), f32)],
        flops=12 * ROWS * D * FF,
        moved=12 * D * FF,
    )(g, x, gain, pre, *w)


def attn_back_kernel(first, d, d_logits, x, gain, g, low_up, low_down, order, w, wt, g_out, gain_out, latent_out, acc):
    h = pl.program_id(0)
    part = jnp.concatenate([dot(d[0], w[0], NT), dot(d[0], wt[0], NT)], axis=1)

    @pl.when(h == 0)
    def _():
        acc[...] = part

    @pl.when(h == 1)
    def _():
        d_latent = dot(d_logits[...], low_up[...], NT, highest)
        latent_out[...] = d_latent
        d_hn = acc[...] + part + dot(d_latent, low_down[...], NT, highest)
        d_v, d_gain = norm_back(x[...], gain[...], d_hn)
        total = g[...] + d_v
        g_out[...] = to_given_order(total, order[...]) if first else total
        gain_out[...] = d_gain


def attn_back(d, d_logits, x, gain, g, low_up, low_down, order, w, place, first):
    return call(
        partial(attn_back_kernel, first),
        (shape(ROWS, D), shape(1, D), shape(ROWS, 16)),
        grid=(2,),
        in_specs=[
            per_half(ROWS, 1536), whole(ROWS, 512), whole(ROWS, D), whole(1, D), whole(ROWS, D),
            whole(16, 512), whole(D, 16), whole(*order.shape),
        ]
        + weight(1536, place),
        out_specs=[whole(ROWS, D), whole(1, D), whole(ROWS, 16)],
        scratch_shapes=[pltpu.VMEM((ROWS, D), f32)],
        flops=4 * ROWS * D * 1536,
        moved=4 * D * 1536,
    )(d, d_logits, x, gain, g, low_up, low_down, order, *w)


def select_kernel(*refs):
    sel, out = refs[-2:]
    for i, a in enumerate(refs[:-2]):
        out[0, i] = dot(a[...], sel[0], NT).astype(bf)


def select(arrays, sel):
    n, count = sel.shape[1], len(arrays)
    both = call(
        select_kernel,
        shape(2, count, ROWS, n, dtype=bf),
        grid=(2,),
        in_specs=[whole(ROWS, D)] * count + [per_half(n, D)],
        out_specs=per_half(count, ROWS, n),
    )(*arrays, sel)
    return both, swap(both)


def own_weight_kernel(a, ar, b, br, d, dr, e, er, out):
    n = d.shape[-1]
    out[0, :, :n] = (dot(a[...], d[0], TN) + dot(ar[...], dr[0], TN)).astype(bf)
    out[0, :, n:] = (dot(b[...], e[0], TN) + dot(br[...], er[0], TN)).astype(bf)


def own_weight(a, ar, d, dr, b, br, e, er):
    n, m = d.shape[-1], e.shape[-1]
    near, far = pl.BlockSpec((ROWS, 512), lambda h: (0, 0)), pl.BlockSpec((ROWS, 512), lambda h: (0, 1))
    return call(
        own_weight_kernel,
        shape(2, 512, n + m, dtype=bf),
        grid=(2,),
        in_specs=[near, far] * 2 + [per_half(ROWS, n)] * 2 + [per_half(ROWS, m)] * 2,
        out_specs=per_half(512, n + m),
    )(a, ar, b, br, d, dr, e, er)


def x_weight_kernel(sets, lead, *refs):
    u, u1, u0 = refs[-3:]
    at = 0
    for i in range(sets):
        a, ar, d, dr = refs[4 * i : 4 * i + 4]
        n = d.shape[-1]
        r = (dot(a[0, 0], d[0], TN) + dot(ar[0, 0], dr[0], TN)).astype(bf)
        to = slice(at, at + n)
        part = lambda i: r[i * 128 : (i + 1) * 128].reshape(lead, 128 // lead, n)
        u[0, :, 0, :, to] = part(0)
        u[1, :, 0, :, to] = part(1)
        u1[:, 0, :, to] = part(2)
        u0[:, 0, :, to] = part(3)
        at += n


def x_weight(group, selected, base, *sets):
    lead = (4, 1)[group]
    total, args, specs = 0, [], []
    for i, (d, dr) in enumerate(sets, base):
        n = d.shape[-1] // 2
        args += [*selected, d, dr]
        specs += [
            pl.BlockSpec((1, 1, ROWS, 512), lambda h, i=i: (0, i, 0, group)),
            pl.BlockSpec((1, 1, ROWS, 512), lambda h, i=i: (1, i, 0, group)),
        ]
        specs += [pl.BlockSpec((1, ROWS, n), lambda h: (h, 0, group))] * 2
        total += n
    dims = (lead, 2, 128 // lead, total)
    return call(
        partial(x_weight_kernel, len(sets), lead),
        (shape(2, *dims, dtype=bf), shape(*dims, dtype=bf), shape(*dims, dtype=bf)),
        grid=(2,),
        in_specs=specs,
        out_specs=[pl.BlockSpec((2, lead, 1, 128 // lead, total), lambda h: (0, 0, h, 0, 0))]
        + [pl.BlockSpec((lead, 1, 128 // lead, total), lambda h: (0, h, 0, 0))] * 2,
        flops=4 * ROWS * D * total,
        moved=2 * D * total,
    )(*args)


def y_weight_kernel(sets, base, where_, *refs):
    u, u1, u0 = refs[-3:]
    h, h2 = where_[0], where_[1]
    at = 0
    for i in range(sets):
        a, ar = refs[:2]
        d, dr = refs[2 * i + 2 : 2 * i + 4]
        n = d.shape[-1]
        to = slice(at, at + n)
        near = lambda place: dot(a[0, base + i, :, :256], d[place], TN) + dot(ar[1, base + i, :, :256], dr[place], TN)
        u0[:, to] = near(h).astype(bf)
        u[0, :, to] = near(1 - h).astype(bf)
        r = (dot(a[0, base + i, :, 256:], d[h2], TN) + dot(ar[1, base + i, :, 256:], dr[h2], TN)).astype(bf)
        u1[:, to] = r[:256]
        u[1, :, to] = r[256:]
        at += n


def y_weight(where_, selected, base, *sets):
    total = sum(d.shape[-1] for d, _ in sets)
    args = [*selected] + [v for pair in sets for v in pair]
    vm = pl.BlockSpec(memory_space=pltpu.VMEM)
    return call(
        partial(y_weight_kernel, len(sets), base),
        (shape(2, 256, total, dtype=bf), shape(256, total, dtype=bf), shape(256, total, dtype=bf)),
        in_specs=[pl.BlockSpec(memory_space=pltpu.SMEM)] + [vm] * len(args),
        out_specs=(vm,) * 3,
        flops=4 * ROWS * D * total,
        moved=2 * D * total,
    )(where_, *args)


def log_sigmoid(v):
    return jnp.minimum(v, 0.0) - jnp.log1p(jnp.exp(-jnp.abs(v)))


def decays(logits):
    ld = log_sigmoid(logits) / decay_norm
    r = lax.broadcasted_iota(jnp.int32, (ROWS, ROWS), 0)
    c = lax.broadcasted_iota(jnp.int32, (ROWS, ROWS), 1)
    lower = ((r >= c) & (r // SPAN == c // SPAN)).astype(f32)
    cum = dot(lower, ld, NN, highest)
    blocks = [cum[i * SPAN : (i + 1) * SPAN] for i in range(4)]
    ends = [b[SPAN - 1 :] for b in blocks]
    return blocks, ends


def run_sum(ends, start, stop):
    total = jnp.zeros_like(ends[0])
    for i in range(start, stop):
        total = total + ends[i]
    return total


def key_factors(blocks, ends, i):
    parts = [jnp.exp((ends[j] - blocks[j]) + run_sum(ends, j + 1, i)) for j in range(i)]
    parts.append(jnp.exp(-blocks[i]))
    return jnp.concatenate(parts, axis=0)


def allowed(segr, segc, i):
    rows_i = segr[i * SPAN : (i + 1) * SPAN]
    count = (i + 1) * SPAN
    r = lax.broadcasted_iota(jnp.int32, (SPAN, count), 0) + i * SPAN
    c = lax.broadcasted_iota(jnp.int32, (SPAN, count), 1)
    return (r >= c) & (rows_i == segc[:, :count])


def start_factors(blocks, ends):
    return jnp.concatenate([jnp.exp(blocks[i] + run_sum(ends, 0, i)) for i in range(4)], axis=0)


def tail_factors(blocks, ends):
    return jnp.concatenate([jnp.exp((ends[i] - blocks[i]) + run_sum(ends, i + 1, 4)) for i in range(4)], axis=0)


def state_kernel(k, v, logits, segr, state):
    blocks, ends = decays(logits[...])
    segr = segr[...]
    tail_k = jnp.where(segr == segr[ROWS - 1 :], k[0].astype(f32) * tail_factors(blocks, ends), 0.0).astype(bf)
    state[0] = dot(tail_k, v[0], TN).astype(bf)


def mix_kernel(q, k, v, logits, segr, segc, out, state_q):
    blocks, ends = decays(logits[...])
    kf = k[0].astype(f32)
    qf = q[0].astype(f32) * scale
    segr, segc = segr[...], segc[...]
    state_q[0] = jnp.where(segr == segr[:1], qf * start_factors(blocks, ends), 0.0).astype(bf)
    for i in range(4):
        count = (i + 1) * SPAN
        qe = (qf[i * SPAN : count] * jnp.exp(blocks[i])).astype(bf)
        ke = (kf[:count] * key_factors(blocks, ends, i)).astype(bf)
        p = jnp.where(allowed(segr, segc, i), dot(qe, ke, NT), 0.0).astype(bf)
        out[0, i * SPAN : count] = dot(p, v[0, :count])


def head_cols(width, first=0):
    return pl.BlockSpec((1, ROWS, width), lambda t: (t // 2, 0, first + t % 2))


def by_head(*dims):
    return pl.BlockSpec((1, *dims), lambda t: (t,) + (0,) * len(dims))


def end_state(qkvg, logits, segr):
    return call(
        state_kernel,
        shape(HEADS, KD, VD, dtype=bf),
        grid=(HEADS,),
        in_specs=[head_cols(KD, 6), head_cols(VD, 1), pl.BlockSpec((ROWS, KD), lambda t: (0, t)), whole(ROWS, 1)],
        out_specs=by_head(KD, VD),
        flops=HEADS * 20_000_000,
        moved=2_000_000,
    )(qkvg, qkvg, logits, segr)


def mix(qkvg, logits, segr, segc):
    return call(
        mix_kernel,
        (shape(2, ROWS, 2 * VD), shape(HEADS, ROWS, KD, dtype=bf)),
        grid=(HEADS,),
        in_specs=[
            head_cols(KD),
            head_cols(KD, 6),
            head_cols(VD, 1),
            pl.BlockSpec((ROWS, KD), lambda t: (0, t)),
            whole(ROWS, 1),
            whole(1, ROWS),
        ],
        out_specs=[head_cols(VD), by_head(ROWS, KD)],
        flops=HEADS * 120_000_000,
        moved=4_000_000,
    )(qkvg, qkvg, qkvg, logits, segr, segc)


def out_weight(place):
    return [pl.BlockSpec((1, 512, VD), lambda t: (t // 2, 0, place * 2 + t % 2))] * 2


def out_kernel(local, state_q, state, g, gain, x, norm_gain, w, wt, mixed_out, rows, x_out, hm_out, acc):
    t = pl.program_id(0)
    mixed = local[0] + dot(state_q[0], state[0])
    mixed_out[0] = mixed
    gate = g[0].astype(f32)
    on = mixed * lax.rsqrt(jnp.mean(mixed * mixed, axis=-1, keepdims=True) + group_eps) * gain[...]
    mine = (on * gate * jax.nn.sigmoid(gate)).astype(bf)
    rows[0] = mine
    part = jnp.concatenate([dot(mine, w[0], NT), dot(mine, wt[0], NT)], axis=1)

    @pl.when(t == 0)
    def _():
        acc[...] = x[...]

    acc[...] += part

    @pl.when(t == HEADS - 1)
    def _():
        total = acc[...]
        x_out[...] = total
        hm_out[...] = rms(total, norm_gain[...]).astype(bf)


def out_rows(local, state_q, state, qkvg, gain, x, norm_gain, w, place):
    return call(
        out_kernel,
        (
            shape(2, ROWS, 2 * VD),
            shape(2, ROWS, 2 * VD, dtype=bf),
            shape(ROWS, D),
            shape(ROWS, D, dtype=bf),
        ),
        grid=(HEADS,),
        in_specs=[
            head_cols(VD), by_head(ROWS, KD), by_head(KD, VD), head_cols(VD, 4), whole(1, VD),
            whole(ROWS, D), whole(1, D),
        ]
        + out_weight(place),
        out_specs=[head_cols(VD), head_cols(VD), whole(ROWS, D), whole(ROWS, D)],
        scratch_shapes=[pltpu.VMEM((ROWS, D), f32)],
        flops=2 * ROWS * D * D + HEADS * 20_000_000,
        moved=2 * D * D + 5_000_000,
    )(local, state_q, state, qkvg, gain, x, norm_gain, *w)


def out_back_kernel(gm, mixed_in, g, gain_in, state_q, w, wt, dg_out, dgain, do_out, d_state):
    dr = dot(gm[:, :512], w[0]) + dot(gm[:, 512:], wt[0])
    mixed = mixed_in[0]
    gate = g[0].astype(f32)
    gain = gain_in[...]
    rho = lax.rsqrt(jnp.mean(mixed * mixed, axis=-1, keepdims=True) + group_eps)
    ng = mixed * rho
    sg = jax.nn.sigmoid(gate)
    d_on = dr * gate * sg
    dg_out[0] = (dr * ng * gain * sg * (1.0 + gate * (1.0 - sg))).astype(bf)
    dgain[0] = jnp.sum(d_on * ng, axis=0, keepdims=True)
    w_ = d_on * gain
    do = (rho * (w_ - ng * jnp.mean(w_ * ng, axis=-1, keepdims=True))).astype(bf)
    do_out[0] = do
    d_state[0] = dot(state_q[0], do, TN).astype(bf)


def out_back(gm, mixed, qkvg, gain, state_q, w, place):
    return call(
        out_back_kernel,
        (
            shape(2, ROWS, 2 * VD, dtype=bf),
            shape(HEADS, 1, VD),
            shape(2, ROWS, 2 * VD, dtype=bf),
            shape(HEADS, KD, VD, dtype=bf),
        ),
        grid=(HEADS,),
        in_specs=[whole(ROWS, D), head_cols(VD), head_cols(VD, 4), whole(1, VD), by_head(ROWS, KD)] + out_weight(place),
        out_specs=[head_cols(VD), by_head(1, VD), head_cols(VD), by_head(KD, VD)],
        flops=2 * ROWS * D * D + HEADS * 20_000_000,
        moved=2 * D * D + 5_000_000,
    )(gm, mixed, qkvg, gain, state_q, *w)


def mix_back_kernel(
    do_in, q, k, v, logits, segr, segc, state_in, state_q_in, dq_out, dk_out, dv_out, net_out
):
    do = do_in[0]
    blocks, ends = decays(logits[...])
    kf = k[0].astype(f32)
    qf = q[0].astype(f32) * scale
    segr, segc = segr[...], segc[...]
    sq = state_q_in[0]
    from_state = dot(do, state_in[0], NT)
    start = jnp.where(segr == segr[:1], start_factors(blocks, ends), 0.0) * scale
    dq_state = from_state * start
    net_state = from_state * sq.astype(f32)
    dk = jnp.zeros((ROWS, KD), f32)
    dv = jnp.zeros((ROWS, VD), f32)
    net_k = jnp.zeros((ROWS, KD), f32)
    nets = []
    grow = lambda a: a if a.shape[0] == ROWS else jnp.concatenate(
        [a, jnp.zeros((ROWS - a.shape[0], a.shape[1]), f32)], axis=0
    )
    for i in range(4):
        count = (i + 1) * SPAN
        here = slice(i * SPAN, count)
        eb = jnp.exp(blocks[i])
        qe = (qf[here] * eb).astype(bf)
        factors = key_factors(blocks, ends, i)
        ke = (kf[:count] * factors).astype(bf)
        keep = allowed(segr, segc, i)
        p = jnp.where(keep, dot(qe, ke, NT), 0.0).astype(bf)
        dp = jnp.where(keep, dot(do[here], v[0, :count], NT), 0.0).astype(bf)
        dv = dv + grow(dot(p, do[here], TN))
        dqe = dot(dp, ke)
        dq_out[0, here] = (dqe * eb * scale + dq_state[here]).astype(bf)
        nets.append(dqe * qe.astype(f32) + net_state[here])
        dke = dot(dp, qe, TN)
        dk = dk + grow(dke * factors)
        net_k = net_k + grow(dke * ke.astype(f32))
    dk_out[0] = dk
    dv_out[0] = dv
    net_out[0] = jnp.concatenate(nets, axis=0) - net_k


def mix_back(do, qkvg, logits, segr, segc, state, state_q):
    return call(
        mix_back_kernel,
        (
            shape(2, ROWS, 2 * KD, dtype=bf),
            shape(HEADS, ROWS, KD),
            shape(HEADS, ROWS, VD),
            shape(HEADS, ROWS, KD),
        ),
        grid=(HEADS,),
        in_specs=[
            head_cols(VD),
            head_cols(KD),
            head_cols(KD, 6),
            head_cols(VD, 1),
            pl.BlockSpec((ROWS, KD), lambda t: (0, t)),
            whole(ROWS, 1),
            whole(1, ROWS),
            by_head(KD, VD),
            by_head(ROWS, KD),
        ],
        out_specs=[head_cols(KD), by_head(ROWS, KD), by_head(ROWS, VD), by_head(ROWS, KD)],
        flops=HEADS * 300_000_000,
        moved=8_000_000,
    )(do, qkvg, qkvg, qkvg, logits, segr, segc, state, state_q)


def decay_back_kernel(dk_in, dv_in, net, k, v, logits_in, segr, segc, d_state, dk_out, dv_out, d_logits):
    logits = logits_in[...]
    blocks, ends = decays(logits)
    segr, segc = segr[...], segc[...]
    kf = k[0].astype(f32)
    tail = jnp.where(segr == segr[ROWS - 1 :], tail_factors(blocks, ends), 0.0)
    tail_k = (kf * tail).astype(bf)
    ds = d_state[0]
    back = dot(v[0], ds, NT)
    dk_out[0] = (dk_in[0] + back * tail).astype(bf)
    dv_out[0] = (dv_in[0] + dot(tail_k, ds)).astype(bf)
    r = lax.broadcasted_iota(jnp.int32, (ROWS, ROWS), 0)
    c = lax.broadcasted_iota(jnp.int32, (ROWS, ROWS), 1)
    same = segr == segc
    after = jnp.where(same & (c >= r), 1.0, 0.0)
    before = jnp.where(same & (c < r), 1.0, 0.0)
    d_ld = dot(after, net[0], NN, highest) + dot(before, back * tail_k.astype(f32), NN, highest)
    d_logits[...] = d_ld * jax.nn.sigmoid(-logits) / decay_norm


def decay_back(dk, dv, net, qkvg, logits, segr, segc, d_state):
    return call(
        decay_back_kernel,
        (
            shape(2, ROWS, 2 * KD, dtype=bf),
            shape(2, ROWS, 2 * VD, dtype=bf),
            shape(ROWS, HEADS * KD),
        ),
        grid=(HEADS,),
        in_specs=[
            by_head(ROWS, KD),
            by_head(ROWS, VD),
            by_head(ROWS, KD),
            head_cols(KD, 6),
            head_cols(VD, 1),
            pl.BlockSpec((ROWS, KD), lambda t: (0, t)),
            whole(ROWS, 1),
            whole(1, ROWS),
            by_head(KD, VD),
        ],
        out_specs=[head_cols(KD), head_cols(VD), pl.BlockSpec((ROWS, KD), lambda t: (0, t))],
        flops=HEADS * 100_000_000,
        moved=4_000_000,
    )(dk, dv, net, qkvg, qkvg, logits, segr, segc, d_state)


def one_hot(places):
    return (places[:, None] == jnp.arange(D, dtype=jnp.int32)[None, :]).astype(bf)


def orders():
    yl, x, z, c, yh = (lax.axis_index(a) for a in FINE)
    k = jnp.arange(D, dtype=jnp.int32)
    base = one_hot((k % 512) // 16 * 32 + jnp.where(k < 512, c, 1 - c) * 16 + k % 16)
    s = 1 - 2 * c
    pick = lambda table, b: jnp.sum(jnp.where(b[:, None] == jnp.arange(table.shape[0])[None], table[None], 0), axis=1)
    far = jnp.array([0, 1, 0, 0, 1, 0, 1, 1], jnp.int32)
    steps = lambda a: jnp.stack([a + 2, a + s, a + s, a, a + 2, a - s, a - s, a]) % 4
    block, r = k // 128, k % 128
    rr = r % 16
    index = lambda far, yl, x, z: far * 512 + ((yl * 4 + x) * 4 + z) * 16 + rr
    along_x = index(pick(far, block), (r // 16) % 2, pick(steps(x), block), r // 32)
    along_z = index(pick(far, block), r // 64, (r // 16) % 4, pick(steps(z), block))
    k = jnp.arange(1536, dtype=jnp.int32)
    block, r = k // 256, k % 256
    rr = r % 16
    along_y = index(
        pick(jnp.array([0, 0, 1, 1, 1, 0], jnp.int32), block),
        pick(jnp.stack([yl, 1 - yl, 1 - yl, yl, 1 - yl, 1 - yl]), block),
        r // 64,
        (r // 16) % 4,
    )
    next_half = ((yh * 2 + yl + s) % 4) // 2
    along_x, along_z, along_y = (a.reshape(2, -1) for a in (along_x, along_z, along_y))
    sel_xz = one_hot(jnp.concatenate([along_x, along_z], axis=1).reshape(-1)).reshape(2, D, D)
    sel_y = one_hot(along_y.reshape(-1)).reshape(2, 768, D)
    return base, sel_xz, sel_y, jnp.stack([yh, next_half]).astype(jnp.int32), jnp.stack([yh * 2 + yl, x, x, z]).astype(jnp.int32)


def own_first(a, axis):
    shape_ = a.shape
    a = a.reshape(*shape_[:axis], 32, 2, 16, *shape_[axis + 1 :])
    zero, one = (lax.index_in_dim(a, i, axis + 1, keepdims=False).reshape(*shape_[:axis], 512, *shape_[axis + 1 :]) for i in (0, 1))
    first = lax.axis_index("c") == 0
    return jnp.concatenate([jnp.where(first, zero, one), jnp.where(first, one, zero)], axis=axis)


def given_order(a, axis):
    shape_ = a.shape
    near, far = lax.slice_in_dim(a, 0, 512, axis=axis), lax.slice_in_dim(a, 512, 1024, axis=axis)
    first = lax.axis_index("c") == 0
    blocks = [b.reshape(*shape_[:axis], 32, 16, *shape_[axis + 1 :]) for b in (jnp.where(first, near, far), jnp.where(first, far, near))]
    return jnp.stack(blocks, axis=axis + 1).reshape(shape_)


def local(
    hidden_in, lengths, cotangent, norm_in, norm_mid, query_w, key_w, value_w, gate_w, out_w,
    low_down, low_up, decay_bias, group_gain, ffn_gate, ffn_up, ffn_down,
):
    yh = lax.axis_index("yh")
    qkvg = [(query_w[l], value_w[l], key_w[l], gate_w[l]) for l in range(LAYERS)]
    feeds = [(ffn_gate[l], ffn_up[l], ffn_down[l]) for l in range(LAYERS)]
    pad = jnp.zeros((16, 128), bf)
    gathered = chip_gather(jnp.concatenate([*qkvg[0], *qkvg[1], out_w[0], out_w[1], pad, *feeds[0]], axis=1))
    gathered_late = chip_gather(jnp.concatenate(feeds[1], axis=1))
    order, sel_xz, sel_y, where_, me = orders()
    bounds = jnp.cumsum(lengths[0])
    places = jnp.arange(ROWS, dtype=jnp.int32) + yh * ROWS
    seg = jnp.sum((places[:, None] >= bounds[None, :]).astype(jnp.int32), axis=1)
    valid = (seg < lengths.shape[1]).astype(f32)
    segr, segc = seg[:, None], seg[None, :]
    gains_in, gains_mid = own_first(norm_in, 1), own_first(norm_mid, 1)
    downs = own_first(low_down, 1)

    x, g, hn = entry(hidden_in, cotangent, valid[:, None], order, gains_in[:1])
    gathered = after(gathered, x, sel_xz, sel_y, gains_in, gains_mid, downs, segr, segc, where_, me)
    first_far = swap(gathered[:, :, :1536])
    gathered = (gathered, swap(after(gathered, first_far)))
    attn_w = [(gathered, 0, 6), (gathered, 1, 7)]
    feed_w = [(gathered, 1), None]
    saved = []
    for layer in range(LAYERS):
        w, at_qkvg, at_out = attn_w[layer]
        qkvg, latent, logits = proj(hn, downs[layer], low_up[layer], decay_bias[layer][None], (w[0], first_far) if layer == 0 else w, at_qkvg, 0 if layer == 0 else at_qkvg)
        state = lax.ppermute(end_state(qkvg, logits, segr), "yh", [(0, 1)])
        local_mix, state_q = mix(qkvg, logits, segr, segc)
        mixed, rows, x_mid, hm = out_rows(
            local_mix, state_q, state, qkvg, group_gain[layer][None], x, gains_mid[layer : layer + 1], w, at_out
        )
        last = layer + 1 == LAYERS
        if last:
            sel_a = select((hn, saved[0][10], saved[0][1]), sel_xz)
            rows_far = [swap(saved[0][8]), swap(rows)]
            acted_far = swap(saved[0][12])
            hm = after(hm, sel_a, rows_far, acted_far)
            gathered_late = after(gathered_late, hm)
            feed_w[1] = ((gathered_late, swap(gathered_late)), 0)
        if last:
            acted, d_pre, output, *back = ffn_both(hm, x_mid, order, g, gains_mid[layer : layer + 1], *feed_w[layer])
            saved.append((x, hn, qkvg, latent, logits, state, state_q, mixed, rows, x_mid, hm, None, acted))
        else:
            pre, acted, x_next, hn_next = ffn(hm, x_mid, gains_in[layer + 1 : layer + 2], *feed_w[layer])
            saved.append((x, hn, qkvg, latent, logits, state, state_q, mixed, rows, x_mid, hm, pre, acted))
            x, hn = x_next, hn_next

    def rings(u):
        return [ring(v[0].reshape(2, 16, 16, -1), a) for v, a in zip(u, "xzy")]

    def second_terms(u, r):
        return add_each(*([(v[1], (w, 0))] for v, w in zip(u, r)))

    def second_rings(t):
        return [ring(sixteens(v), a) for v, a in zip(t, "xzy")]

    def small_grads(grad_in, grad_mid, hn, d_latent, latent, d_logits, d_gain):
        return (
            grad_in,
            grad_mid,
            dot(hn.astype(f32), d_latent, TN, highest),
            dot(latent, d_logits, TN, highest),
            jnp.sum(d_logits, axis=0),
            jnp.sum(d_gain[:, 0], axis=0),
        )

    def flatten(small):
        stacked = [jnp.stack([part[i] for part in small]) for i in range(6)]
        for i in range(3):
            stacked[i] = given_order(stacked[i], 1)
        flat = jnp.concatenate([a.reshape(-1) for a in stacked])
        return stacked, jnp.pad(flat, (0, 32 * 2944 - flat.shape[0])).reshape(32, 2944)

    then = Order()
    small = [None] * LAYERS
    for layer in reversed(range(LAYERS)):
        x, hn, qkvg, latent, logits, state, state_q, mixed, rows, x_mid, hm, pre, acted = saved[layer]
        bottom = layer == 0
        w, at_qkvg, at_out = attn_w[layer]
        if bottom:
            d_pre, *back = then(ffn_back, g, x_mid, gains_mid[layer : layer + 1], pre, *feed_w[layer])
        gb, g_mid, gm, grad_mid = back
        d_pre_far = swap(d_pre)
        d_g, d_gain, do, d_state = then(out_back, gm, mixed, qkvg, group_gain[layer][None], state_q, w, at_out)
        d_state = lax.ppermute(d_state, "yh", [(1, 0)])
        if bottom:
            sel_b = then(select, (gm_above, gb, gm), sel_y)
        else:
            t = then(own_weight, hm, swap(hm), d_pre, d_pre_far, gb, swap(gb), acted, swap(acted))
            top = lax.psum_scatter(t.reshape(64, 16, 3 * FF), CHIPS, scatter_dimension=0, tiled=False)
        d_q, d_k, d_v, net = then(mix_back, do, qkvg, logits, segr, segc, state, state_q)
        d_k, d_v, d_logits = then(decay_back, d_k, d_v, net, qkvg, logits, segr, segc, d_state)
        d = jnp.concatenate([d_q, d_v, d_k, d_g], axis=2)
        d_far = swap(d)
        if bottom:
            sets = (d_above, d_above_far), (d_pre, d_pre_far), (d, d_far)
            u = [
                then(lambda v: x_weight(0, sel_a, 0, *v), sets),
                then(lambda v: x_weight(1, sel_a, 0, *v), sets),
                then(lambda v: y_weight(where_, sel_b, 0, *v), ((rows_above, rows_far[1]), (acted, acted_far), (rows, rows_far[0]))),
            ]
            r = rings(u)
        else:
            d_above, d_above_far, gm_above, rows_above = d, d_far, gm, rows
        g, grad_in, d_latent = then(
            attn_back,
            d, d_logits, x, gains_in[layer : layer + 1], g_mid, low_up[layer], downs[layer].astype(f32), order, w, at_qkvg, bottom
        )
        small[layer] = (grad_in[0], grad_mid[0], hn, d_latent, latent, d_logits, d_gain)
        if bottom:
            stacked, flat = flatten([small_grads(*after(v, u)) for v in small])
            flat = flat + swap(flat)
            flat = flat.astype(bf)
            moved = [shift(flat, "z", j) for j in (1, 2, 3)]
            r_far = [swap(v) for v in r]
            t1 = then(second_terms, u, after(r, flat, r_far))
            r1 = second_rings(t1)
    input_grad = g

    parts = [[(u[i][2], r1[i], (r_far[i], 1))] for i in range(3)]
    (whole_x,) = add_each([(after(u[0][2], moved), r1[0], (r_far[0], 1))])
    flat = [flat] + moved
    got_x = lax.all_to_all(sixteens(whole_x), ("z", "yh", "yl"), 0, 0, tiled=True)
    parts = split_sums(after(me[:2], whole_x), 64, parts[1:], flat, 0)
    parts = [passed_on(p, a) for p, a in zip(parts, "yx")]
    parts = after(parts, got_x)
    parts = split_sums(me[2:], 16, [[p] for p in parts], parts[0], 2)
    parts = [passed_on(p, a) for p, a in zip(parts, "xz")]
    *grads, total = final_sums(got_x, parts[0], parts[1], top)
    total = total.reshape(-1)
    small_sums, at = [], 0
    for a in stacked:
        small_sums.append(total[at : at + a.size].reshape(a.shape))
        at += a.size

    return (
        output,
        input_grad,
        small_sums[0],
        small_sums[1],
        *grads[:5],
        small_sums[2],
        small_sums[3],
        small_sums[4],
        small_sums[5],
        *grads[5:],
    )


def solution(mesh):
    fine = Mesh(mesh.devices.reshape(2, 4, 4, 2, 2), FINE)
    dp = ("yl", "x", "z", "c")
    every = P(FINE, None)
    mat = P(None, dp, "yh")
    rep = P()
    in_specs = (every, P(dp, None), every, rep, rep) + (mat,) * 5 + (rep,) * 4 + (mat,) * 3
    out_specs = (every, every, rep, rep) + (mat,) * 5 + (rep,) * 4 + (mat,) * 3
    return jax.shard_map(local, mesh=fine, in_specs=in_specs, out_specs=out_specs, check_vma=False)
```

```python
from functools import partial

import jax
import jax.numpy as jnp
from jax import lax
from jax.experimental import pallas as pl
from jax.experimental.pallas import tpu as pltpu
from jax.sharding import Mesh, PartitionSpec as P

LAYERS = 2
HEADS = 4
SPAN = 64
ATT = 2048
FF = 1408
ROWS = 256
D = 1024
KD = 128
VD = 256
FINE = ("yl", "x", "z", "c", "yh")
CHIPS = ("yh", "yl", "x", "z")
bf = jnp.bfloat16
f32 = jnp.float32
highest = lax.Precision.HIGHEST
norm_eps = 1e-06
group_eps = 1.0
decay_norm = 16.0
scale = KD**-0.5
NN = (((1,), (0,)), ((), ()))
NT = (((1,), (1,)), ((), ()))
TN = (((0,), (0,)), ((), ()))


def dot(a, b, dims=NN, precision=None):
    return lax.dot_general(a, b, dims, precision=precision, preferred_element_type=f32)


def call(kernel, out_shape, *, flops=500_000_000, moved=8_000_000, vmem=48, **kw):
    return pl.pallas_call(
        kernel,
        out_shape=out_shape,
        compiler_params=pltpu.CompilerParams(vmem_limit_bytes=vmem << 20),
        cost_estimate=pl.CostEstimate(flops=flops, bytes_accessed=moved, transcendentals=0),
        **kw,
    )


def shape(*dims, dtype=f32):
    return jax.ShapeDtypeStruct(dims, dtype)


def swap(a):
    return lax.ppermute(a, "c", [(0, 1), (1, 0)])


def ring(a, axis, cross=0):
    if axis == "y":
        names = ("yl", "c", "yh")
        place = lambda i, c: ((i % 2) * 2 + c) * 2 + i // 2
    else:
        names = (axis, "c")
        place = lambda i, c: i * 2 + c
    pairs = [
        (place(i, c), place((i + 1 - 2 * c) % 4, c ^ cross)) for i in range(4) for c in range(2)
    ]
    return lax.ppermute(a, names, pairs)


def shift(a, axis, step):
    if axis == "y":
        place = lambda i: (i % 2) * 2 + i // 2
        return lax.ppermute(a, ("yl", "yh"), [(place(i), place((i + step) % 4)) for i in range(4)])
    return lax.ppermute(a, axis, [(i, (i + step) % 4) for i in range(4)])


def chip_gather(s):
    return lax.all_gather(s, CHIPS, axis=0, tiled=True).reshape(2, 512, s.shape[1])


def after(value, *others):
    return lax.optimization_barrier((value, others))[0]


def rows_part(t, start, n):
    v = t[...].reshape(t.shape[-2:])
    return (v if v.shape[1] == n else v[:, start : start + n]).astype(f32)


def add_kernel(plan, *refs):
    at = sum(count for _, count, _, _ in plan)
    outs, place = refs[at:], 0
    for out, count, start, n in plan:
        value = sum(rows_part(t, start, n) for t in refs[place : place + count])
        outs[out][:, start : start + n] = value.astype(bf)
        place += count


def add_each(*groups):
    args, specs, outs, out_specs, plan, moved = [], [], [], [], [], 0
    for group in groups:
        start = 0
        for terms in group:
            for term in terms:
                a, which = term if isinstance(term, tuple) else (term, None)
                wide = a.shape[-1]
                if which is None:
                    args.append(a.reshape(256, wide))
                    specs.append(pl.BlockSpec((64, wide), lambda i: (i, 0)))
                else:
                    args.append(a.reshape(2, 256, wide))
                    specs.append(pl.BlockSpec((1, 64, wide), lambda i, which=which: (which, i, 0)))
            n = terms[0].shape[-1]
            plan.append((len(outs), len(terms), start, n))
            start += n
            moved += 512 * n * (len(terms) + 1)
        outs.append(shape(256, start, dtype=bf))
        out_specs.append(pl.BlockSpec((64, start), lambda i: (i, 0)))
    return call(
        partial(add_kernel, plan), tuple(outs), grid=(4,), in_specs=specs, out_specs=out_specs, flops=0, moved=0
    )(*args)


def split_kernel(plan, rows, extra, me, *refs):
    i = pl.program_id(0)
    at = sum(count for _, count, _, _ in plan) + extra
    outs, place = refs[at:], extra
    added = sum(t[...].astype(f32) for t in refs[:extra]).astype(bf)
    for group, count, start, n in plan:
        value = sum(rows_part(t, start, n) for t in refs[place : place + count]).astype(bf)
        place += count
        for j in range(4):

            @pl.when(i == j)
            def _(out=outs[4 * group + j], value=value, start=start, n=n, group=group):
                out[:rows, start : start + n] = value
                if group == 0:
                    out[rows:, start : start + n] = added[:, start : start + n]


def split_sums(me, rows, groups, extra, extra_place):
    args, specs, outs, out_specs, plan = [], [], [], [], []
    for a in extra:
        args.append(a)
        specs.append(pl.BlockSpec((32, a.shape[1]), lambda i, me: (extra_place, 0)))
    for g, group in enumerate(groups):
        start = 0
        for terms in group:
            for term in terms:
                a, which = term if isinstance(term, tuple) else (term, None)
                wide = a.shape[-1]
                if which is None:
                    args.append(a.reshape(-1, wide))
                    specs.append(pl.BlockSpec((rows, wide), lambda i, me, g=g: ((me[g] + i) % 4, 0)))
                else:
                    args.append(a.reshape(2, 4 * rows, wide))
                    specs.append(pl.BlockSpec((1, rows, wide), lambda i, me, g=g, which=which: (which, (me[g] + i) % 4, 0)))
            n = terms[0].shape[-1]
            plan.append((g, len(terms), start, n))
            start += n
        dims = (rows + (32 if g == 0 else 0), start)
        outs += [shape(*dims, dtype=bf)] * 4
        out_specs += [pl.BlockSpec(dims, lambda i, me: (0, 0))] * 4
    out = call(
        partial(split_kernel, plan, rows, len(extra)),
        tuple(outs),
        flops=0,
        moved=0,
        grid_spec=pltpu.PrefetchScalarGridSpec(num_scalar_prefetch=1, grid=(4,), in_specs=specs, out_specs=out_specs),
    )(me, *args)
    return [out[4 * g : 4 * g + 4] for g in range(len(groups))]


def final_kernel(x, *refs):
    z, y, top = refs[:4], refs[4:8], refs[8]
    outs = refs[9:]
    groups = [sum(x[i].astype(f32) for i in range(16))]
    groups += [sum(t[...].astype(f32) for t in g) for g in (z, y)]
    outs[8][...] = groups[1][16:]
    for out, g, lo, hi in ((0, 0, 0, 256), (1, 1, 0, 256), (2, 0, 256, 768), (3, 1, 256, 768), (4, 2, 0, 512)):
        mine = groups[g].shape[1] - (512 if g == 2 else 768)
        outs[out][0] = groups[g][:16, mine + lo : mine + hi]
        outs[out][1] = groups[g][:16, lo:hi]
    for g in range(3):
        at = 512 if g == 2 else 768
        outs[5 + g][0] = groups[g][:16, at : at + FF]
        outs[5 + g][1] = top[:, g * FF : (g + 1) * FF].astype(f32)


def final_sums(x, z, y, top):
    widths = (256, 256, 512, 512, 512, FF, FF, FF)
    return call(final_kernel, tuple(shape(2, 16, w) for w in widths) + (shape(32, z[0].shape[1]),))(x, *z, *y, top)


def passed_on(blocks, axis):
    return [blocks[0]] + [shift(blocks[j], axis, j) for j in (1, 2, 3)]


class Order:
    def __init__(self):
        self.seen = ()

    def __call__(self, kernel, first, *rest):
        out = kernel(after(first, *self.seen), *rest)
        self.seen = (out,)
        return out


def sixteens(a):
    return a.reshape(16, 16, a.shape[-1])


def whole(*dims):
    return pl.BlockSpec(dims, lambda h: (0,) * len(dims))


def per_half(*dims):
    return pl.BlockSpec((1, *dims), lambda h: (h,) + (0,) * len(dims))


def weight(width, place, far_place=None):
    far_place = place if far_place is None else far_place
    return [pl.BlockSpec((1, 512, width), lambda h, p=p: (h, 0, p)) for p in (place, far_place)]


def rms(v, gain):
    return v * lax.rsqrt(jnp.mean(v * v, axis=-1, keepdims=True) + norm_eps) * gain


def norm_back(v, gain, d_out):
    r = lax.rsqrt(jnp.mean(v * v, axis=-1, keepdims=True) + norm_eps)
    u = d_out * gain
    d_v = r * u - v * (r * r * r) * jnp.mean(u * v, axis=-1, keepdims=True)
    return d_v, jnp.sum(d_out * v * r, axis=0, keepdims=True)


def to_given_order(value, order):
    high = value.astype(bf)
    rest = value - high.astype(f32)
    mid = rest.astype(bf)
    low = (rest - mid.astype(f32)).astype(bf)
    return dot(high, order) + dot(mid, order) + dot(low, order)


def entry_kernel(hidden, cot, valid, order, gain, x_out, g_out, hn_out):
    x = dot(hidden[...], order[...], NT)
    x_out[...] = x
    g_out[...] = dot(cot[...], order[...], NT) * valid[...]
    hn_out[...] = rms(x, gain[...]).astype(bf)


def entry(hidden, cot, valid, order, gain):
    return call(
        entry_kernel,
        (shape(ROWS, D), shape(ROWS, D), shape(ROWS, D, dtype=bf)),
        flops=4 * ROWS * D * D,
        moved=8 * D * D,
    )(hidden, cot, valid, order, gain)


def proj_kernel(hn, low_down, low_up, bias, w, wt, out, latent_out, logits_out):
    out[0] = (dot(hn[:, :512], w[0]) + dot(hn[:, 512:], wt[0])).astype(bf)

    @pl.when(pl.program_id(0) == 0)
    def _():
        latent = dot(hn[...], low_down[...])
        latent_out[...] = latent
        logits_out[...] = dot(latent, low_up[...], NN, highest) + bias[...]


def proj(hn, low_down, low_up, bias, w, place, far_place):
    return call(
        proj_kernel,
        (shape(2, ROWS, 1536, dtype=bf), shape(ROWS, 16), shape(ROWS, 512)),
        grid=(2,),
        in_specs=[whole(ROWS, D), whole(D, 16), whole(16, 512), whole(1, 512)] + weight(1536, place, far_place),
        out_specs=[per_half(ROWS, 1536), whole(ROWS, 16), whole(ROWS, 512)],
        flops=4 * ROWS * D * 1536,
        moved=4 * D * 1536,
    )(hn, low_down, low_up, bias, *w)


def ffn_kernel(hm, x, gain, w, wt, pre_out, acted_out, x_out, hn_out, acc):
    h = pl.program_id(0)
    near, far = hm[:, :512], hm[:, 512:]
    gate = dot(near, w[0, :, :FF]) + dot(far, wt[0, :, :FF])
    up = dot(near, w[0, :, FF : 2 * FF]) + dot(far, wt[0, :, FF : 2 * FF])
    pre_out[0, :, :FF] = gate.astype(bf)
    pre_out[0, :, FF:] = up.astype(bf)
    acted = (gate * jax.nn.sigmoid(gate) * up).astype(bf)
    acted_out[0] = acted
    part = jnp.concatenate([dot(acted, w[0, :, 2 * FF :], NT), dot(acted, wt[0, :, 2 * FF :], NT)], axis=1)

    @pl.when(h == 0)
    def _():
        acc[...] = part

    @pl.when(h == 1)
    def _():
        total = x[...] + (acc[...] + part)
        x_out[...] = total
        hn_out[...] = rms(total, gain[...]).astype(bf)


def ffn(hm, x, gain, w, place):
    return call(
        ffn_kernel,
        (
            shape(2, ROWS, 2 * FF, dtype=bf),
            shape(2, ROWS, FF, dtype=bf),
            shape(ROWS, D),
            shape(ROWS, D, dtype=bf),
        ),
        grid=(2,),
        in_specs=[whole(ROWS, D), whole(ROWS, D), whole(1, D)] + weight(3 * FF, place),
        out_specs=[per_half(ROWS, 2 * FF), per_half(ROWS, FF), whole(ROWS, D), whole(ROWS, D)],
        scratch_shapes=[pltpu.VMEM((ROWS, D), f32)],
        flops=12 * ROWS * D * FF,
        moved=12 * D * FF,
    )(hm, x, gain, *w)


def ffn_both_kernel(
    hm, x, order, g, gain, w, wt, acted_out, d_out, x_out, gb_out, g_out, gm_out, gain_out, acc, acc_back
):
    h = pl.program_id(0)
    near, far = hm[:, :512], hm[:, 512:]
    gate = dot(near, w[0, :, :FF]) + dot(far, wt[0, :, :FF])
    up = dot(near, w[0, :, FF : 2 * FF]) + dot(far, wt[0, :, FF : 2 * FF])
    sg = jax.nn.sigmoid(gate)
    acted = (gate * sg * up).astype(bf)
    acted_out[0] = acted
    part = jnp.concatenate([dot(acted, w[0, :, 2 * FF :], NT), dot(acted, wt[0, :, 2 * FF :], NT)], axis=1)
    gb = g[...].astype(bf)
    da = dot(gb[:, :512], w[0, :, 2 * FF :]) + dot(gb[:, 512:], wt[0, :, 2 * FF :])
    d_gate = (da * up * sg * (1.0 + gate * (1.0 - sg))).astype(bf)
    d_up = (da * gate * sg).astype(bf)
    d_out[0, :, :FF] = d_gate
    d_out[0, :, FF:] = d_up
    back = jnp.concatenate(
        [dot(d_gate, v[0, :, :FF], NT) + dot(d_up, v[0, :, FF : 2 * FF], NT) for v in (w, wt)], axis=1
    )

    @pl.when(h == 0)
    def _():
        acc[...] = part
        acc_back[...] = back
        gb_out[...] = gb

    @pl.when(h == 1)
    def _():
        x_out[...] = to_given_order(x[...] + (acc[...] + part), order[...])
        d_v, d_gain = norm_back(x[...], gain[...], acc_back[...] + back)
        total = g[...] + d_v
        g_out[...] = total
        gm_out[...] = total.astype(bf)
        gain_out[...] = d_gain


def ffn_both(hm, x, order, g, gain, w, place):
    return call(
        ffn_both_kernel,
        (
            shape(2, ROWS, FF, dtype=bf),
            shape(2, ROWS, 2 * FF, dtype=bf),
            shape(ROWS, D),
            shape(ROWS, D, dtype=bf),
            shape(ROWS, D),
            shape(ROWS, D, dtype=bf),
            shape(1, D),
        ),
        grid=(2,),
        in_specs=[whole(ROWS, D), whole(ROWS, D), whole(D, D), whole(ROWS, D), whole(1, D)] + weight(3 * FF, place),
        out_specs=[
            per_half(ROWS, FF), per_half(ROWS, 2 * FF), whole(ROWS, D), whole(ROWS, D), whole(ROWS, D),
            whole(ROWS, D), whole(1, D),
        ],
        scratch_shapes=[pltpu.VMEM((ROWS, D), f32)] * 2,
        flops=24 * ROWS * D * FF,
        moved=12 * D * FF,
    )(hm, x, order, g, gain, *w)


def ffn_back_kernel(g, x, gain, pre, w, wt, d_out, gb_out, g_out, gm_out, gain_out, acc):
    h = pl.program_id(0)
    gb = g[...].astype(bf)
    da = dot(gb[:, :512], w[0, :, 2 * FF :]) + dot(gb[:, 512:], wt[0, :, 2 * FF :])
    gate = pre[0, :, :FF].astype(f32)
    up = pre[0, :, FF:].astype(f32)
    sg = jax.nn.sigmoid(gate)
    d_gate = (da * up * sg * (1.0 + gate * (1.0 - sg))).astype(bf)
    d_up = (da * gate * sg).astype(bf)
    d_out[0, :, :FF] = d_gate
    d_out[0, :, FF:] = d_up
    part = jnp.concatenate(
        [
            dot(d_gate, v[0, :, :FF], NT) + dot(d_up, v[0, :, FF : 2 * FF], NT)
            for v in (w, wt)
        ],
        axis=1,
    )

    @pl.when(h == 0)
    def _():
        acc[...] = part
        gb_out[...] = gb

    @pl.when(h == 1)
    def _():
        d_v, d_gain = norm_back(x[...], gain[...], acc[...] + part)
        total = g[...] + d_v
        g_out[...] = total
        gm_out[...] = total.astype(bf)
        gain_out[...] = d_gain


def ffn_back(g, x, gain, pre, w, place):
    return call(
        ffn_back_kernel,
        (
            shape(2, ROWS, 2 * FF, dtype=bf),
            shape(ROWS, D, dtype=bf),
            shape(ROWS, D),
            shape(ROWS, D, dtype=bf),
            shape(1, D),
        ),
        grid=(2,),
        in_specs=[whole(ROWS, D), whole(ROWS, D), whole(1, D), per_half(ROWS, 2 * FF)] + weight(3 * FF, place),
        out_specs=[per_half(ROWS, 2 * FF), whole(ROWS, D), whole(ROWS, D), whole(ROWS, D), whole(1, D)],
        scratch_shapes=[pltpu.VMEM((ROWS, D), f32)],
        flops=12 * ROWS * D * FF,
        moved=12 * D * FF,
    )(g, x, gain, pre, *w)


def attn_back_kernel(first, d, d_logits, x, gain, g, low_up, low_down, order, w, wt, g_out, gain_out, latent_out, acc):
    h = pl.program_id(0)
    part = jnp.concatenate([dot(d[0], w[0], NT), dot(d[0], wt[0], NT)], axis=1)

    @pl.when(h == 0)
    def _():
        acc[...] = part

    @pl.when(h == 1)
    def _():
        d_latent = dot(d_logits[...], low_up[...], NT, highest)
        latent_out[...] = d_latent
        d_hn = acc[...] + part + dot(d_latent, low_down[...], NT, highest)
        d_v, d_gain = norm_back(x[...], gain[...], d_hn)
        total = g[...] + d_v
        g_out[...] = to_given_order(total, order[...]) if first else total
        gain_out[...] = d_gain


def attn_back(d, d_logits, x, gain, g, low_up, low_down, order, w, place, first):
    return call(
        partial(attn_back_kernel, first),
        (shape(ROWS, D), shape(1, D), shape(ROWS, 16)),
        grid=(2,),
        in_specs=[
            per_half(ROWS, 1536), whole(ROWS, 512), whole(ROWS, D), whole(1, D), whole(ROWS, D),
            whole(16, 512), whole(D, 16), whole(*order.shape),
        ]
        + weight(1536, place),
        out_specs=[whole(ROWS, D), whole(1, D), whole(ROWS, 16)],
        scratch_shapes=[pltpu.VMEM((ROWS, D), f32)],
        flops=0 if first else 4 * ROWS * D * 1536,
        moved=0 if first else 4 * D * 1536,
    )(d, d_logits, x, gain, g, low_up, low_down, order, *w)


def select_kernel(*refs):
    sel, out = refs[-2:]
    for i, a in enumerate(refs[:-2]):
        out[0, i] = dot(a[...], sel[0], NT).astype(bf)


def select(arrays, sel):
    n, count = sel.shape[1], len(arrays)
    both = call(
        select_kernel,
        shape(2, count, ROWS, n, dtype=bf),
        grid=(2,),
        in_specs=[whole(ROWS, D)] * count + [per_half(n, D)],
        out_specs=per_half(count, ROWS, n),
    )(*arrays, sel)
    return both, swap(both)


def own_weight_kernel(a, ar, b, br, d, dr, e, er, out):
    n = d.shape[-1]
    out[0, :, :n] = (dot(a[...], d[0], TN) + dot(ar[...], dr[0], TN)).astype(bf)
    out[0, :, n:] = (dot(b[...], e[0], TN) + dot(br[...], er[0], TN)).astype(bf)


def own_weight(a, ar, d, dr, b, br, e, er):
    n, m = d.shape[-1], e.shape[-1]
    near, far = pl.BlockSpec((ROWS, 512), lambda h: (0, 0)), pl.BlockSpec((ROWS, 512), lambda h: (0, 1))
    return call(
        own_weight_kernel,
        shape(2, 512, n + m, dtype=bf),
        grid=(2,),
        in_specs=[near, far] * 2 + [per_half(ROWS, n)] * 2 + [per_half(ROWS, m)] * 2,
        out_specs=per_half(512, n + m),
    )(a, ar, b, br, d, dr, e, er)


def x_weight_kernel(sets, lead, *refs):
    outs = refs[-4:]
    at = 0
    for i in range(sets):
        a, ar, d, dr = refs[4 * i : 4 * i + 4]
        n = d.shape[-1]
        r = (dot(a[0, 0], d[0], TN) + dot(ar[0, 0], dr[0], TN)).astype(bf)
        to = slice(at, at + n)
        part = lambda i: r[i * 128 : (i + 1) * 128].reshape(lead, 128 // lead, n)
        for k, out in enumerate(outs):
            out[:, 0, :, to] = part(k)
        at += n


def x_weight(group, selected, base, *sets):
    lead = (4, 1)[group]
    total, args, specs = 0, [], []
    for i, (d, dr) in enumerate(sets, base):
        n = d.shape[-1] // 2
        args += [*selected, d, dr]
        specs += [
            pl.BlockSpec((1, 1, ROWS, 512), lambda h, i=i: (0, i, 0, group)),
            pl.BlockSpec((1, 1, ROWS, 512), lambda h, i=i: (1, i, 0, group)),
        ]
        specs += [pl.BlockSpec((1, ROWS, n), lambda h: (h, 0, group))] * 2
        total += n
    dims = (lead, 2, 128 // lead, total)
    return call(
        partial(x_weight_kernel, len(sets), lead),
        (shape(*dims, dtype=bf),) * 4,
        grid=(2,),
        in_specs=specs,
        out_specs=[pl.BlockSpec((lead, 1, 128 // lead, total), lambda h: (0, h, 0, 0))] * 4,
        flops=0,
        moved=0,
    )(*args)


def y_weight_kernel(sets, base, where_, *refs):
    u2, u1b, u1, u0 = refs[-4:]
    h, h2 = where_[0], where_[1]
    at = 0
    for i in range(sets):
        a, ar = refs[:2]
        d, dr = refs[2 * i + 2 : 2 * i + 4]
        n = d.shape[-1]
        to = slice(at, at + n)
        near = lambda place: dot(a[0, base + i, :, :256], d[place], TN) + dot(ar[1, base + i, :, :256], dr[place], TN)
        u0[:, to] = near(h).astype(bf)
        u2[:, to] = near(1 - h).astype(bf)
        r = (dot(a[0, base + i, :, 256:], d[h2], TN) + dot(ar[1, base + i, :, 256:], dr[h2], TN)).astype(bf)
        u1[:, to] = r[:256]
        u1b[:, to] = r[256:]
        at += n


def y_weight(where_, selected, base, *sets):
    total = sum(d.shape[-1] for d, _ in sets)
    args = [*selected] + [v for pair in sets for v in pair]
    vm = pl.BlockSpec(memory_space=pltpu.VMEM)
    return call(
        partial(y_weight_kernel, len(sets), base),
        (shape(256, total, dtype=bf),) * 4,
        in_specs=[pl.BlockSpec(memory_space=pltpu.SMEM)] + [vm] * len(args),
        out_specs=(vm,) * 4,
        flops=0,
        moved=0,
    )(where_, *args)


def exact(picks, v):
    high = v.astype(bf)
    rest = v - high.astype(f32)
    mid = rest.astype(bf)
    low = (rest - mid.astype(f32)).astype(bf)
    return dot(picks, high) + dot(picks, mid) + dot(picks, low)


def log_sigmoid(v):
    return jnp.minimum(v, 0.0) - jnp.log1p(jnp.exp(-jnp.abs(v)))


def cumulative(logits):
    ld = log_sigmoid(logits) / decay_norm
    r = lax.broadcasted_iota(jnp.int32, (ROWS, ROWS), 0)
    c = lax.broadcasted_iota(jnp.int32, (ROWS, ROWS), 1)
    lower = ((r >= c) & (r // SPAN == c // SPAN)).astype(f32)
    return exact(lower.astype(bf), ld)


def decays(cum):
    blocks = [cum[i * SPAN : (i + 1) * SPAN] for i in range(4)]
    ends = [b[SPAN - 1 :] for b in blocks]
    return blocks, ends


def run_sum(ends, start, stop):
    total = jnp.zeros_like(ends[0])
    for i in range(start, stop):
        total = total + ends[i]
    return total


def key_factors(blocks, ends, i):
    parts = [jnp.exp((ends[j] - blocks[j]) + run_sum(ends, j + 1, i)) for j in range(i)]
    parts.append(jnp.exp(-blocks[i]))
    return jnp.concatenate(parts, axis=0)


def allowed(segr, segc, i):
    rows_i = segr[i * SPAN : (i + 1) * SPAN]
    count = (i + 1) * SPAN
    r = lax.broadcasted_iota(jnp.int32, (SPAN, count), 0) + i * SPAN
    c = lax.broadcasted_iota(jnp.int32, (SPAN, count), 1)
    return (r >= c) & (rows_i == segc[:, :count])


def start_factors(blocks, ends):
    return jnp.concatenate([jnp.exp(blocks[i] + run_sum(ends, 0, i)) for i in range(4)], axis=0)


def tail_factors(blocks, ends):
    return jnp.concatenate([jnp.exp((ends[i] - blocks[i]) + run_sum(ends, i + 1, 4)) for i in range(4)], axis=0)


def state_kernel(k, v, logits, segr, state, cum_out):
    cum = cumulative(logits[...])
    cum_out[...] = cum
    blocks, ends = decays(cum)
    segr = segr[...]
    tail_k = jnp.where(segr == segr[ROWS - 1 :], k[0].astype(f32) * tail_factors(blocks, ends), 0.0).astype(bf)
    state[0] = dot(tail_k, v[0], TN).astype(bf)


def mix_kernel(q, k, v, cum, segr, segc, out, state_q):
    blocks, ends = decays(cum[...])
    kf = k[0].astype(f32)
    qf = q[0].astype(f32) * scale
    segr, segc = segr[...], segc[...]
    state_q[0] = jnp.where(segr == segr[:1], qf * start_factors(blocks, ends), 0.0).astype(bf)
    for i in range(4):
        count = (i + 1) * SPAN
        qe = (qf[i * SPAN : count] * jnp.exp(blocks[i])).astype(bf)
        ke = (kf[:count] * key_factors(blocks, ends, i)).astype(bf)
        p = jnp.where(allowed(segr, segc, i), dot(qe, ke, NT), 0.0).astype(bf)
        out[0, i * SPAN : count] = dot(p, v[0, :count])


def head_cols(width, first=0):
    return pl.BlockSpec((1, ROWS, width), lambda t: (t // 2, 0, first + t % 2))


def by_head(*dims):
    return pl.BlockSpec((1, *dims), lambda t: (t,) + (0,) * len(dims))


def end_state(qkvg, logits, segr):
    return call(
        state_kernel,
        (shape(HEADS, KD, VD, dtype=bf), shape(ROWS, HEADS * KD)),
        grid=(HEADS,),
        in_specs=[head_cols(KD, 6), head_cols(VD, 1), pl.BlockSpec((ROWS, KD), lambda t: (0, t)), whole(ROWS, 1)],
        out_specs=[by_head(KD, VD), pl.BlockSpec((ROWS, KD), lambda t: (0, t))],
        flops=HEADS * 20_000_000,
        moved=2_000_000,
    )(qkvg, qkvg, logits, segr)


def mix(qkvg, logits, segr, segc):
    return call(
        mix_kernel,
        (shape(2, ROWS, 2 * VD), shape(HEADS, ROWS, KD, dtype=bf)),
        grid=(HEADS,),
        in_specs=[
            head_cols(KD),
            head_cols(KD, 6),
            head_cols(VD, 1),
            pl.BlockSpec((ROWS, KD), lambda t: (0, t)),
            whole(ROWS, 1),
            whole(1, ROWS),
        ],
        out_specs=[head_cols(VD), by_head(ROWS, KD)],
        flops=HEADS * 120_000_000,
        moved=4_000_000,
    )(qkvg, qkvg, qkvg, logits, segr, segc)


def out_weight(place):
    return [pl.BlockSpec((1, 512, VD), lambda t: (t // 2, 0, place * 2 + t % 2))] * 2


def out_kernel(local, state_q, state, g, gain, x, norm_gain, w, wt, mixed_out, rows, x_out, hm_out, acc):
    t = pl.program_id(0)
    mixed = local[0] + dot(state_q[0], state[0])
    mixed_out[0] = mixed
    gate = g[0].astype(f32)
    on = mixed * lax.rsqrt(jnp.mean(mixed * mixed, axis=-1, keepdims=True) + group_eps) * gain[...]
    mine = (on * gate * jax.nn.sigmoid(gate)).astype(bf)
    rows[0] = mine
    part = jnp.concatenate([dot(mine, w[0], NT), dot(mine, wt[0], NT)], axis=1)

    @pl.when(t == 0)
    def _():
        acc[...] = x[...]

    acc[...] += part

    @pl.when(t == HEADS - 1)
    def _():
        total = acc[...]
        x_out[...] = total
        hm_out[...] = rms(total, norm_gain[...]).astype(bf)


def out_rows(local, state_q, state, qkvg, gain, x, norm_gain, w, place):
    return call(
        out_kernel,
        (
            shape(2, ROWS, 2 * VD),
            shape(2, ROWS, 2 * VD, dtype=bf),
            shape(ROWS, D),
            shape(ROWS, D, dtype=bf),
        ),
        grid=(HEADS,),
        in_specs=[
            head_cols(VD), by_head(ROWS, KD), by_head(KD, VD), head_cols(VD, 4), whole(1, VD),
            whole(ROWS, D), whole(1, D),
        ]
        + out_weight(place),
        out_specs=[head_cols(VD), head_cols(VD), whole(ROWS, D), whole(ROWS, D)],
        scratch_shapes=[pltpu.VMEM((ROWS, D), f32)],
        flops=2 * ROWS * D * D + HEADS * 20_000_000,
        moved=2 * D * D + 5_000_000,
    )(local, state_q, state, qkvg, gain, x, norm_gain, *w)


def out_back_kernel(gm, mixed_in, g, gain_in, state_q, w, wt, dg_out, dgain, do_out, d_state):
    dr = dot(gm[:, :512], w[0]) + dot(gm[:, 512:], wt[0])
    mixed = mixed_in[0]
    gate = g[0].astype(f32)
    gain = gain_in[...]
    rho = lax.rsqrt(jnp.mean(mixed * mixed, axis=-1, keepdims=True) + group_eps)
    ng = mixed * rho
    sg = jax.nn.sigmoid(gate)
    d_on = dr * gate * sg
    dg_out[0] = (dr * ng * gain * sg * (1.0 + gate * (1.0 - sg))).astype(bf)
    dgain[0] = jnp.sum(d_on * ng, axis=0, keepdims=True)
    w_ = d_on * gain
    do = (rho * (w_ - ng * jnp.mean(w_ * ng, axis=-1, keepdims=True))).astype(bf)
    do_out[0] = do
    d_state[0] = dot(state_q[0], do, TN).astype(bf)


def out_back(gm, mixed, qkvg, gain, state_q, w, place):
    return call(
        out_back_kernel,
        (
            shape(2, ROWS, 2 * VD, dtype=bf),
            shape(HEADS, 1, VD),
            shape(2, ROWS, 2 * VD, dtype=bf),
            shape(HEADS, KD, VD, dtype=bf),
        ),
        grid=(HEADS,),
        in_specs=[whole(ROWS, D), head_cols(VD), head_cols(VD, 4), whole(1, VD), by_head(ROWS, KD)] + out_weight(place),
        out_specs=[head_cols(VD), by_head(1, VD), head_cols(VD), by_head(KD, VD)],
        flops=2 * ROWS * D * D + HEADS * 20_000_000,
        moved=2 * D * D + 5_000_000,
    )(gm, mixed, qkvg, gain, state_q, *w)


def mix_back_kernel(
    do_in, q, k, v, cum, segr, segc, state_in, state_q_in, dq_out, dk_out, dv_out, net_out
):
    do = do_in[0]
    blocks, ends = decays(cum[...])
    kf = k[0].astype(f32)
    qf = q[0].astype(f32) * scale
    segr, segc = segr[...], segc[...]
    sq = state_q_in[0]
    from_state = dot(do, state_in[0], NT)
    start = jnp.where(segr == segr[:1], start_factors(blocks, ends), 0.0) * scale
    dq_state = from_state * start
    net_state = from_state * sq.astype(f32)
    dk = jnp.zeros((ROWS, KD), f32)
    dv = jnp.zeros((ROWS, VD), f32)
    net_k = jnp.zeros((ROWS, KD), f32)
    nets = []
    grow = lambda a: a if a.shape[0] == ROWS else jnp.concatenate(
        [a, jnp.zeros((ROWS - a.shape[0], a.shape[1]), f32)], axis=0
    )
    for i in range(4):
        count = (i + 1) * SPAN
        here = slice(i * SPAN, count)
        eb = jnp.exp(blocks[i])
        qe = (qf[here] * eb).astype(bf)
        factors = key_factors(blocks, ends, i)
        ke = (kf[:count] * factors).astype(bf)
        keep = allowed(segr, segc, i)
        p = jnp.where(keep, dot(qe, ke, NT), 0.0).astype(bf)
        dp = jnp.where(keep, dot(do[here], v[0, :count], NT), 0.0).astype(bf)
        dv = dv + grow(dot(p, do[here], TN))
        dqe = dot(dp, ke)
        dq_out[0, here] = (dqe * eb * scale + dq_state[here]).astype(bf)
        nets.append(dqe * qe.astype(f32) + net_state[here])
        dke = dot(dp, qe, TN)
        dk = dk + grow(dke * factors)
        net_k = net_k + grow(dke * ke.astype(f32))
    dk_out[0] = dk
    dv_out[0] = dv
    net_out[0] = jnp.concatenate(nets, axis=0) - net_k


def mix_back(do, qkvg, logits, segr, segc, state, state_q):
    return call(
        mix_back_kernel,
        (
            shape(2, ROWS, 2 * KD, dtype=bf),
            shape(HEADS, ROWS, KD),
            shape(HEADS, ROWS, VD),
            shape(HEADS, ROWS, KD),
        ),
        grid=(HEADS,),
        in_specs=[
            head_cols(VD),
            head_cols(KD),
            head_cols(KD, 6),
            head_cols(VD, 1),
            pl.BlockSpec((ROWS, KD), lambda t: (0, t)),
            whole(ROWS, 1),
            whole(1, ROWS),
            by_head(KD, VD),
            by_head(ROWS, KD),
        ],
        out_specs=[head_cols(KD), by_head(ROWS, KD), by_head(ROWS, VD), by_head(ROWS, KD)],
        flops=HEADS * 300_000_000,
        moved=8_000_000,
    )(do, qkvg, qkvg, qkvg, logits, segr, segc, state, state_q)


def decay_back_kernel(dk_in, dv_in, net, k, v, logits_in, cum, segr, segc, d_state, dk_out, dv_out, d_logits):
    logits = logits_in[...]
    blocks, ends = decays(cum[...])
    segr, segc = segr[...], segc[...]
    kf = k[0].astype(f32)
    tail = jnp.where(segr == segr[ROWS - 1 :], tail_factors(blocks, ends), 0.0)
    tail_k = (kf * tail).astype(bf)
    ds = d_state[0]
    back = dot(v[0], ds, NT)
    dk_out[0] = (dk_in[0] + back * tail).astype(bf)
    dv_out[0] = (dv_in[0] + dot(tail_k, ds)).astype(bf)
    r = lax.broadcasted_iota(jnp.int32, (ROWS, ROWS), 0)
    c = lax.broadcasted_iota(jnp.int32, (ROWS, ROWS), 1)
    same = segr == segc
    after = jnp.where(same & (c >= r), 1.0, 0.0).astype(bf)
    before = jnp.where(same & (c < r), 1.0, 0.0).astype(bf)
    d_ld = exact(after, net[0]) + exact(before, back * tail_k.astype(f32))
    d_logits[...] = d_ld * jax.nn.sigmoid(-logits) / decay_norm


def decay_back(dk, dv, net, qkvg, logits, cum, segr, segc, d_state):
    return call(
        decay_back_kernel,
        (
            shape(2, ROWS, 2 * KD, dtype=bf),
            shape(2, ROWS, 2 * VD, dtype=bf),
            shape(ROWS, HEADS * KD),
        ),
        grid=(HEADS,),
        in_specs=[
            by_head(ROWS, KD),
            by_head(ROWS, VD),
            by_head(ROWS, KD),
            head_cols(KD, 6),
            head_cols(VD, 1),
            pl.BlockSpec((ROWS, KD), lambda t: (0, t)),
            pl.BlockSpec((ROWS, KD), lambda t: (0, t)),
            whole(ROWS, 1),
            whole(1, ROWS),
            by_head(KD, VD),
        ],
        out_specs=[head_cols(KD), head_cols(VD), pl.BlockSpec((ROWS, KD), lambda t: (0, t))],
        flops=HEADS * 100_000_000,
        moved=4_000_000,
    )(dk, dv, net, qkvg, qkvg, logits, cum, segr, segc, d_state)


def one_hot(places):
    return (places[:, None] == jnp.arange(D, dtype=jnp.int32)[None, :]).astype(bf)


def orders():
    yl, x, z, c, yh = (lax.axis_index(a) for a in FINE)
    k = jnp.arange(D, dtype=jnp.int32)
    base = one_hot((k % 512) // 16 * 32 + jnp.where(k < 512, c, 1 - c) * 16 + k % 16)
    s = 1 - 2 * c
    pick = lambda table, b: jnp.sum(jnp.where(b[:, None] == jnp.arange(table.shape[0])[None], table[None], 0), axis=1)
    far = jnp.array([0, 1, 0, 0, 1, 0, 1, 1], jnp.int32)
    steps = lambda a: jnp.stack([a + 2, a + s, a + s, a, a + 2, a - s, a - s, a]) % 4
    block, r = k // 128, k % 128
    rr = r % 16
    index = lambda far, yl, x, z: far * 512 + ((yl * 4 + x) * 4 + z) * 16 + rr
    along_x = index(pick(far, block), (r // 16) % 2, pick(steps(x), block), r // 32)
    along_z = index(pick(far, block), r // 64, (r // 16) % 4, pick(steps(z), block))
    k = jnp.arange(1536, dtype=jnp.int32)
    block, r = k // 256, k % 256
    rr = r % 16
    along_y = index(
        pick(jnp.array([0, 0, 1, 1, 1, 0], jnp.int32), block),
        pick(jnp.stack([yl, 1 - yl, 1 - yl, yl, 1 - yl, 1 - yl]), block),
        r // 64,
        (r // 16) % 4,
    )
    next_half = ((yh * 2 + yl + s) % 4) // 2
    along_x, along_z, along_y = (a.reshape(2, -1) for a in (along_x, along_z, along_y))
    sel_xz = one_hot(jnp.concatenate([along_x, along_z], axis=1).reshape(-1)).reshape(2, D, D)
    sel_y = one_hot(along_y.reshape(-1)).reshape(2, 768, D)
    return base, sel_xz, sel_y, jnp.stack([yh, next_half]).astype(jnp.int32), jnp.stack([yh * 2 + yl, x, x, z]).astype(jnp.int32)


def own_first(a, axis):
    shape_ = a.shape
    a = a.reshape(*shape_[:axis], 32, 2, 16, *shape_[axis + 1 :])
    zero, one = (lax.index_in_dim(a, i, axis + 1, keepdims=False).reshape(*shape_[:axis], 512, *shape_[axis + 1 :]) for i in (0, 1))
    first = lax.axis_index("c") == 0
    return jnp.concatenate([jnp.where(first, zero, one), jnp.where(first, one, zero)], axis=axis)


def given_order(a, axis):
    shape_ = a.shape
    near, far = lax.slice_in_dim(a, 0, 512, axis=axis), lax.slice_in_dim(a, 512, 1024, axis=axis)
    first = lax.axis_index("c") == 0
    blocks = [b.reshape(*shape_[:axis], 32, 16, *shape_[axis + 1 :]) for b in (jnp.where(first, near, far), jnp.where(first, far, near))]
    return jnp.stack(blocks, axis=axis + 1).reshape(shape_)


def local(
    hidden_in, lengths, cotangent, norm_in, norm_mid, query_w, key_w, value_w, gate_w, out_w,
    low_down, low_up, decay_bias, group_gain, ffn_gate, ffn_up, ffn_down,
):
    yh = lax.axis_index("yh")
    qkvg = [(query_w[l], value_w[l], key_w[l], gate_w[l]) for l in range(LAYERS)]
    feeds = [(ffn_gate[l], ffn_up[l], ffn_down[l]) for l in range(LAYERS)]
    pad = jnp.zeros((16, 128), bf)
    gathered = chip_gather(jnp.concatenate([*qkvg[0], *qkvg[1], out_w[0], out_w[1], pad, *feeds[0]], axis=1))
    gathered_late = chip_gather(jnp.concatenate(feeds[1], axis=1))
    order, sel_xz, sel_y, where_, me = orders()
    bounds = jnp.cumsum(lengths[0])
    places = jnp.arange(ROWS, dtype=jnp.int32) + yh * ROWS
    seg = jnp.sum((places[:, None] >= bounds[None, :]).astype(jnp.int32), axis=1)
    valid = (seg < lengths.shape[1]).astype(f32)
    segr, segc = seg[:, None], seg[None, :]
    gains_in, gains_mid = own_first(norm_in, 1), own_first(norm_mid, 1)
    downs = own_first(low_down, 1)

    x, g, hn = entry(hidden_in, cotangent, valid[:, None], order, gains_in[:1])
    gathered = after(gathered, x, sel_xz, sel_y, gains_in, gains_mid, downs, segr, segc, where_, me)
    first_far = swap(gathered[:, :, :1536])
    gathered = (gathered, swap(after(gathered, first_far)))
    attn_w = [(gathered, 0, 6), (gathered, 1, 7)]
    feed_w = [(gathered, 1), None]
    saved = []
    for layer in range(LAYERS):
        w, at_qkvg, at_out = attn_w[layer]
        qkvg, latent, logits = proj(hn, downs[layer], low_up[layer], decay_bias[layer][None], (w[0], first_far) if layer == 0 else w, at_qkvg, 0 if layer == 0 else at_qkvg)
        state, cum = end_state(qkvg, logits, segr)
        state = lax.ppermute(state, "yh", [(0, 1)])
        local_mix, state_q = mix(qkvg, cum, segr, segc)
        mixed, rows, x_mid, hm = out_rows(
            local_mix, state_q, state, qkvg, group_gain[layer][None], x, gains_mid[layer : layer + 1], w, at_out
        )
        last = layer + 1 == LAYERS
        if last:
            sel_a = select((hn, saved[0][10], saved[0][1]), sel_xz)
            rows_far = [swap(saved[0][8]), swap(rows)]
            acted_far = swap(saved[0][12])
            hm = after(hm, sel_a, rows_far, acted_far)
            gathered_late = after(gathered_late, hm)
            feed_w[1] = ((gathered_late, swap(gathered_late)), 0)
        if last:
            acted, d_pre, output, *back = ffn_both(hm, x_mid, order, g, gains_mid[layer : layer + 1], *feed_w[layer])
            saved.append((x, hn, qkvg, latent, (logits, cum), state, state_q, mixed, rows, x_mid, hm, None, acted))
        else:
            pre, acted, x_next, hn_next = ffn(hm, x_mid, gains_in[layer + 1 : layer + 2], *feed_w[layer])
            saved.append((x, hn, qkvg, latent, (logits, cum), state, state_q, mixed, rows, x_mid, hm, pre, acted))
            x, hn = x_next, hn_next

    def rings(u):
        return [ring(sixteens(v[0]), a) for v, a in zip(u, "xzy")]

    def second_terms(u, r):
        return add_each(*([(v[2], w)] for v, w in zip(u, r)))

    def second_rings(t, moved):
        t = t[0], after(t[1], moved), t[2]
        return [ring(sixteens(v), a) for v, a in zip(t, "xzy")]

    def small_grads(grad_in, grad_mid, hn, d_latent, latent, d_logits, d_gain):
        return (
            grad_in,
            grad_mid,
            dot(hn.astype(f32), d_latent, TN, highest),
            dot(latent, d_logits, TN, highest),
            jnp.sum(d_logits, axis=0),
            jnp.sum(d_gain[:, 0], axis=0),
        )

    def flatten(small):
        stacked = [jnp.stack([part[i] for part in small]) for i in range(6)]
        for i in range(3):
            stacked[i] = given_order(stacked[i], 1)
        flat = jnp.concatenate([a.reshape(-1) for a in stacked])
        return stacked, jnp.pad(flat, (0, 32 * 2944 - flat.shape[0])).reshape(32, 2944)

    then = Order()
    small = [None] * LAYERS
    for layer in reversed(range(LAYERS)):
        x, hn, qkvg, latent, (logits, cum), state, state_q, mixed, rows, x_mid, hm, pre, acted = saved[layer]
        bottom = layer == 0
        w, at_qkvg, at_out = attn_w[layer]
        if bottom:
            d_pre, *back = then(ffn_back, g, x_mid, gains_mid[layer : layer + 1], pre, *feed_w[layer])
        gb, g_mid, gm, grad_mid = back
        d_pre_far = swap(d_pre)
        d_g, d_gain, do, d_state = then(out_back, gm, mixed, qkvg, group_gain[layer][None], state_q, w, at_out)
        d_state = lax.ppermute(d_state, "yh", [(1, 0)])
        if bottom:
            sel_b = then(select, (gm_above, gb, gm), sel_y)
        else:
            t = then(own_weight, hm, swap(hm), d_pre, d_pre_far, gb, swap(gb), acted, swap(acted))
            top = lax.psum_scatter(t.reshape(64, 16, 3 * FF), CHIPS, scatter_dimension=0, tiled=False)
        d_q, d_k, d_v, net = then(mix_back, do, qkvg, cum, segr, segc, state, state_q)
        d_k, d_v, d_logits = then(decay_back, d_k, d_v, net, qkvg, logits, cum, segr, segc, d_state)
        d = jnp.concatenate([d_q, d_v, d_k, d_g], axis=2)
        d_far = swap(d)
        if bottom:
            sets = (d_above, d_above_far), (d_pre, d_pre_far), (d, d_far)
            u = [
                then(lambda v: x_weight(0, sel_a, 0, *v), sets),
                then(lambda v: x_weight(1, sel_a, 0, *v), sets),
                then(lambda v: y_weight(where_, sel_b, 0, *v), ((rows_above, rows_far[1]), (acted, acted_far), (rows, rows_far[0]))),
            ]
            r = rings(u)
            r_far = [ring(sixteens(v[1]), a, 1) for v, a in zip(u, "xzy")]
        else:
            d_above, d_above_far, gm_above, rows_above = d, d_far, gm, rows
        g, grad_in, d_latent = then(
            attn_back,
            d, d_logits, x, gains_in[layer : layer + 1], g_mid, low_up[layer], downs[layer].astype(f32), order, w, at_qkvg, bottom
        )
        small[layer] = (grad_in[0], grad_mid[0], hn, d_latent, latent, d_logits, d_gain)
        if bottom:
            stacked, flat = flatten([small_grads(*after(v, r)) for v in small])
            flat = flat + swap(flat)
            flat = flat.astype(bf)
            moved = [shift(flat, "z", j) for j in (1, 2, 3)]
            t1 = then(second_terms, u, after(r, flat))
            r1 = second_rings(t1, moved)
    input_grad = g

    parts = [[(u[i][3], r1[i], r_far[i])] for i in range(3)]
    (whole_x,) = add_each(parts[0])
    flat = [flat] + moved
    got_x = lax.all_to_all(sixteens(whole_x), ("z", "yh", "yl"), 0, 0, tiled=True)
    parts = split_sums(after(me[:2], whole_x), 64, parts[1:], flat, 0)
    parts = [passed_on(p, a) for p, a in zip(parts, "yx")]
    parts = after(parts, got_x)
    parts = split_sums(me[2:], 16, [[p] for p in parts], parts[0], 2)
    parts = [passed_on(p, a) for p, a in zip(parts, "xz")]
    *grads, total = final_sums(got_x, parts[0], parts[1], top)
    total = total.reshape(-1)
    small_sums, at = [], 0
    for a in stacked:
        small_sums.append(total[at : at + a.size].reshape(a.shape))
        at += a.size

    return (
        output,
        input_grad,
        small_sums[0],
        small_sums[1],
        *grads[:5],
        small_sums[2],
        small_sums[3],
        small_sums[4],
        small_sums[5],
        *grads[5:],
    )


def solution(mesh):
    fine = Mesh(mesh.devices.reshape(2, 4, 4, 2, 2), FINE)
    dp = ("yl", "x", "z", "c")
    every = P(FINE, None)
    mat = P(None, dp, "yh")
    rep = P()
    in_specs = (every, P(dp, None), every, rep, rep) + (mat,) * 5 + (rep,) * 4 + (mat,) * 3
    out_specs = (every, every, rep, rep) + (mat,) * 5 + (rep,) * 4 + (mat,) * 3
    return jax.shard_map(local, mesh=fine, in_specs=in_specs, out_specs=out_specs, check_vma=False)
```
